32 devices in a mesh: tgt: 8 (over z, x), band: 4 (over y, core).
Axes of the slice: x: 2, y: 2, z: 4, core: 2. Of those that a mesh axis runs over, the one named last changes fastest.
Arguments:
- exposure_flux: bfloat16 [1024, 4096], P('tgt', 'band'), may hold values from -6 to 6
- exposure_ivar: bfloat16 [1024, 4096], P('tgt', 'band'), may hold values from 0.19921875 to 5
- exposure_res: bfloat16 [1024, 11, 4096], P('tgt', None, 'band'), may hold values from 0 to 1
- target_of_row: int32 [1024], replicated, may hold values from 0 to 127, as said below
- valid_of_row: int32 [1024], replicated, may hold values from 0 to 1, as said below
- rest_basis: float32 [10, 4608], replicated, may hold values from -6 to 6
- redshift_shift: int32 [32], replicated, may hold values from 0 to 511
Outputs:
- coadd_flux: float32 [128, 4096], P('tgt', 'band')
- coadd_res: bfloat16 [128, 11, 4096], P('tgt', None, 'band')
- fit_gain: float32 [128, 32], P('tgt', 'band')
The draws below stay inside these ranges and needn't reach their ends.
Inputs may be any that keep to these rules, and one draw needn't show every extreme that they name: `target_of_row`: every target has exactly 8 rows. The rows held by one index of tgt (rows j * 128 to (j + 1) * 128 - 1) include at most 32 rows of the targets of any one owner, where the owner of target t is t // 16; some pairs reach 32. `valid_of_row`: every target has at least one row with flag 1.
All inputs are finite; a program needn't handle non-finite values.
Results may differ from the reference program's by a relative error of at most 0.004.
Values may be sent and summed in bfloat16 or wider, within the bound.
A program may use at most 128 MiB of HBM per device.

```python
import math
import jax
import jax.numpy as jnp
import numpy as np
from jax import lax

TGT_DEV = 16
SLOTS = 8
NDIAG = 11
NB = 10
SHIFT = 512
OWNERS = 8
TARGETS = 128
EXP_DEV = 128
EXPOSURES = 1024
CAP = 32
NW = 4096
NZ = 32
NREST = 4608


def routing(key):
    owners = OWNERS
    row_count = EXP_DEV
    capacity = CAP
    key_order, key_slots, key_rows, key_first, key_coin = jax.random.split(key, 5)
    rank_of = jnp.argsort(jax.random.permutation(key_order, owners)).astype(jnp.int32)
    values = jnp.arange(owners, dtype=jnp.int32)
    score = jnp.where(values == owners - 1, -3, jnp.where(values == 1, -2, jnp.where(values == owners // 2, -1, rank_of)))
    offset_order = jnp.argsort(score, stable=True).astype(jnp.int32)
    slot_ids = jnp.arange(row_count, dtype=jnp.int32)
    half_rows = row_count // 2
    groups = jnp.where(slot_ids < half_rows, slot_ids // capacity, owners // 4 + (slot_ids - half_rows) // (capacity // 2))
    offsets = offset_order[groups]

    def one_receiver(slot_key):
        return jax.random.permutation(slot_key, row_count)
    slot_order = jax.vmap(one_receiver)(jax.random.split(key_slots, owners))
    slot_offset = offsets[slot_order]
    receiver = jnp.arange(owners, dtype=jnp.int32)[:, None]
    source = (receiver + slot_offset) % owners
    rank_order = jax.random.permutation(key_rows, owners * row_count).astype(jnp.int32)
    sort_keys = source.reshape(-1).astype(jnp.int32) * (owners * row_count) + rank_order
    row_order = jnp.argsort(sort_keys)
    flat_ids = jnp.arange(owners * row_count, dtype=jnp.int32)
    receiver_flat = flat_ids // row_count
    slot_flat = flat_ids % row_count
    target = receiver_flat * TGT_DEV + slot_flat // SLOTS
    first_valid = jax.random.randint(key_first, (owners * TGT_DEV,), 0, SLOTS)
    coin_flip = jax.random.randint(key_coin, (owners * row_count,), 0, 10)
    valid_flag = jnp.logical_or(slot_flat % SLOTS == first_valid[target], coin_flip < 6)
    return (target[row_order].astype(jnp.int32), valid_flag[row_order].astype(jnp.int32))


def draw_target_of_row(key, part):
    return routing(key)[0]


def draw_valid_of_row(key, part):
    return routing(key)[1]


def place_ends(values, own_key, smallest, largest):
    dims = values.shape
    spot = [jax.random.randint(jax.random.fold_in(own_key, axis), (), 0, dims[axis]) for axis in range(len(dims))]
    values = values.at[tuple(spot)].set(smallest)
    longest = dims.index(max(dims))
    spot[longest] = (spot[longest] + 1) % dims[longest]
    return values.at[tuple(spot)].set(largest)


def levels(stream_key, dims, shards, least, largest):
    level, own = 1.0, jax.random.fold_in(stream_key, 6)
    for position, shards_of in shards:
        draws = jnp.exp(jax.random.uniform(jax.random.fold_in(own, position), (shards_of,), jnp.float32, least / len(shards), largest / len(shards)))
        level = level * jnp.repeat(draws, dims[position] // shards_of).reshape([-1 if axis == position else 1 for axis in range(len(dims))])
    return level


def noise(rng, shape, spread, limit, cuts=(), kind=jnp.bfloat16):
    level = levels(rng, shape, cuts, -0.22, 0.18) if cuts else 1.0
    result = jax.random.normal(rng, shape, jnp.float32) * spread * level
    return jnp.minimum(jnp.maximum(result, -limit), limit).astype(kind)


def setup_inputs(seed: int = 0) -> dict:
    seeds = jax.random.split(jax.random.key(seed), 8)
    return {
        "exposure_flux": noise(seeds[0], (EXPOSURES, NW), 1.0, 6.0, ((0, 8), (1, 4))),
        "exposure_ivar": jnp.clip(jnp.exp(math.log(5.0) - 3.2227897 * jax.random.uniform(seeds[1], (EXPOSURES, NW), jnp.float32) ** levels(seeds[1], (EXPOSURES, NW), ((0, 8), (1, 4)), -0.2, 0.2)), 0.19921875, 5.0).astype(jnp.bfloat16),
        "exposure_res": jnp.clip(1.0 * jax.random.uniform(seeds[2], (EXPOSURES, NDIAG, NW), jnp.float32) ** levels(seeds[2], (EXPOSURES, NDIAG, NW), ((0, 8), (2, 4)), -0.2, 0.2), 0.0, 1.0).astype(jnp.bfloat16),
        "target_of_row": draw_target_of_row(jax.random.fold_in(seeds[7], 71), 0),
        "valid_of_row": draw_valid_of_row(jax.random.fold_in(seeds[7], 71), 0),
        "rest_basis": noise(seeds[5], (NB, NREST), 1.0, 6.0, (), jnp.float32),
        "redshift_shift": place_ends(jax.random.randint(seeds[6], (NZ,), 0, SHIFT), jax.random.fold_in(seeds[6], 1), 0, SHIFT - 1).astype(jnp.int32),
    }


pair_first, pair_second = np.triu_indices(10)


def solve_normal(matrix, right_side):
    basis_count = right_side.shape[0]
    rows_of = [[None] * basis_count for column in range(basis_count)]
    for p in range(len(pair_first)):
        b = int(pair_first[p])
        c = int(pair_second[p])
        rows_of[b][c] = matrix[p]
        rows_of[c][b] = matrix[p]
    vector = [right_side[b] for b in range(basis_count)]
    for k in range(basis_count):
        inverse = 1.0 / rows_of[k][k]
        for r in range(k + 1, basis_count):
            factor = rows_of[r][k] * inverse
            for c in range(k + 1, basis_count):
                rows_of[r][c] = rows_of[r][c] - factor * rows_of[k][c]
            vector[r] = vector[r] - factor * vector[k]
    answer = [None] * basis_count
    for k in reversed(range(basis_count)):
        running = vector[k]
        for c in range(k + 1, basis_count):
            running = running - rows_of[k][c] * answer[c]
        answer[k] = running / rows_of[k][k]
    gain_total = right_side[0] * answer[0]
    for b in range(1, basis_count):
        gain_total = gain_total + right_side[b] * answer[b]
    return gain_total


def basis_windows(rest_basis, shifts, first_wave, length):
    def one_shift(shift_value):
        return lax.dynamic_slice_in_dim(rest_basis, (first_wave + shift_value).astype(jnp.int32), length, axis=1)
    return jax.vmap(one_shift)(shifts)


def normal_terms(weight_sum, flux_sum, windows):
    products = windows[:, pair_first, :] * windows[:, pair_second, :]
    matrix = jnp.einsum('ti,zpi->ztp', weight_sum, products, precision=lax.Precision.HIGHEST)
    right_side = jnp.einsum('ti,zbi->ztb', flux_sum, windows, precision=lax.Precision.HIGHEST)
    return matrix, right_side


def blocked_normals(weight_sum, flux_sum, rest_basis, shifts, first_wave, length):
    total_shifts = shifts.shape[0]
    block_size = 8 if total_shifts % 8 == 0 else total_shifts
    grouped = shifts.reshape(total_shifts // block_size, block_size)

    def one_block(shift_block):
        return normal_terms(weight_sum, flux_sum, basis_windows(rest_basis, shift_block, first_wave, length))

    matrix, right_side = lax.map(one_block, grouped)
    return (matrix.reshape((total_shifts,) + matrix.shape[2:]),
            right_side.reshape((total_shifts,) + right_side.shape[2:]))


def fit_from(matrix, right_side):
    pairs = jnp.transpose(matrix, (2, 0, 1)).reshape(matrix.shape[2], -1)
    sides = jnp.transpose(right_side, (2, 0, 1)).reshape(right_side.shape[2], -1)
    gain = solve_normal(pairs, sides).reshape(matrix.shape[0], matrix.shape[1])
    return gain.T


def reference(exposure_flux, exposure_ivar, exposure_res, target_of_row, valid_of_row, rest_basis, redshift_shift):
    weight = exposure_ivar.astype(jnp.float32) * valid_of_row.astype(jnp.float32)[:, None]
    weight_sum = jax.ops.segment_sum(weight, target_of_row, num_segments=TARGETS)
    flux_sum = jax.ops.segment_sum(weight * exposure_flux.astype(jnp.float32), target_of_row, num_segments=TARGETS)
    block_rows = EXP_DEV * 4
    block_total = EXPOSURES // block_rows
    res_blocks = exposure_res.reshape(block_total, block_rows, NDIAG, NW)
    weight_blocks = weight.reshape(block_total, block_rows, NW)
    target_blocks = target_of_row.reshape(block_total, block_rows)

    def add_block(carry, pieces):
        res_piece, weight_piece, target_piece = pieces
        update = weight_piece[:, None, :] * res_piece.astype(jnp.float32)
        return carry.at[target_piece].add(update), None

    res_sum, unused = lax.scan(add_block, jnp.zeros((TARGETS, NDIAG, NW), jnp.float32),
                               (res_blocks, weight_blocks, target_blocks))
    coadd_flux = flux_sum / weight_sum
    coadd_res = (res_sum / weight_sum[:, None, :]).astype(jnp.bfloat16)
    matrix, right_side = blocked_normals(weight_sum, flux_sum, rest_basis, redshift_shift, 0, NW)
    fit_gain = fit_from(matrix, right_side)
    return coadd_flux, coadd_res, fit_gain
```

```python
import functools

import jax
import jax.numpy as jnp
import numpy as np
from jax import lax
from jax.experimental import pallas as pl
from jax.experimental.pallas import tpu as pltpu
from jax.sharding import PartitionSpec as P

TGT_DEV = 16
NDIAG = 11
Z_DEV = 8
PIECE_LANES = 128
FIT_LANES = 256
AHEAD = 2
VMEM_LIMIT = 48 * 1024 * 1024
MESH = pl.DeviceIdType.MESH


pair_first, pair_second = np.triu_indices(10)


def solve_normal(matrix, right_side):
    basis_count = right_side.shape[0]
    rows_of = [[None] * basis_count for column in range(basis_count)]
    for p in range(len(pair_first)):
        b = int(pair_first[p])
        c = int(pair_second[p])
        rows_of[b][c] = matrix[p]
        rows_of[c][b] = matrix[p]
    vector = [right_side[b] for b in range(basis_count)]
    for k in range(basis_count):
        inverse = 1.0 / rows_of[k][k]
        for r in range(k + 1, basis_count):
            factor = rows_of[r][k] * inverse
            for c in range(k + 1, basis_count):
                rows_of[r][c] = rows_of[r][c] - factor * rows_of[k][c]
            vector[r] = vector[r] - factor * vector[k]
    answer = [None] * basis_count
    for k in reversed(range(basis_count)):
        running = vector[k]
        for c in range(k + 1, basis_count):
            running = running - rows_of[k][c] * answer[c]
        answer[k] = running / rows_of[k][k]
    gain_total = right_side[0] * answer[0]
    for b in range(1, basis_count):
        gain_total = gain_total + right_side[b] * answer[b]
    return gain_total


def basis_windows(rest_basis, shifts, first_wave, length):

    def one_shift(shift_value):
        return lax.dynamic_slice_in_dim(rest_basis, first_wave + shift_value, length, axis=1)

    return jax.vmap(one_shift)(shifts)


def normal_terms(weight_sum, flux_sum, windows):
    products = windows[:, pair_first, :] * windows[:, pair_second, :]
    matrix = jnp.einsum("ti,zpi->ztp", weight_sum, products, precision=lax.Precision.HIGHEST)
    right_side = jnp.einsum("ti,zbi->ztb", flux_sum, windows, precision=lax.Precision.HIGHEST)
    return (matrix, right_side)


def blocked_normals(weight_sum, flux_sum, rest_basis, shifts, first_wave, length):
    total_shifts = shifts.shape[0]
    block_size = 8
    grouped = shifts.reshape(total_shifts // block_size, block_size)

    def one_block(shift_block):
        return normal_terms(
            weight_sum, flux_sum, basis_windows(rest_basis, shift_block, first_wave, length)
        )

    matrix, right_side = lax.map(one_block, grouped)
    return (
        matrix.reshape((total_shifts,) + matrix.shape[2:]),
        right_side.reshape((total_shifts,) + right_side.shape[2:]),
    )


def fit_from(matrix, right_side):
    pairs = jnp.transpose(matrix, (2, 0, 1)).reshape(matrix.shape[2], -1)
    sides = jnp.transpose(right_side, (2, 0, 1)).reshape(right_side.shape[2], -1)
    gain = solve_normal(pairs, sides).reshape(matrix.shape[0], matrix.shape[1])
    return gain.T


def shards(
    exposure_flux,
    exposure_ivar,
    exposure_res,
    target_of_row,
    valid_of_row,
    rest_basis,
    redshift_shift,
):
    owners = lax.axis_size("tgt")
    device = lax.axis_index("tgt")
    row_count = exposure_flux.shape[0]
    wave_dev = exposure_flux.shape[1]
    capacity = 2 * row_count // owners
    own_target = lax.dynamic_slice_in_dim(target_of_row, device * row_count, row_count)
    owner_of = own_target // TGT_DEV
    row_ids = jnp.arange(row_count, dtype=jnp.int32)
    earlier = row_ids[None, :] < row_ids[:, None]
    position = jnp.sum(jnp.logical_and(owner_of[:, None] == owner_of[None, :], earlier), axis=1)
    slot_index = owner_of * capacity + position
    source_row = jnp.full((owners * capacity,), row_count, jnp.int32).at[slot_index].set(row_ids)

    def packed(values):
        gathered = jnp.take(values, source_row, axis=0, mode="fill", fill_value=0)
        return gathered.reshape((owners, capacity) + values.shape[1:])

    target_table = target_of_row.reshape(owners, row_count)
    is_mine = (target_table // TGT_DEV == device).astype(jnp.int32)
    before = jnp.cumsum(is_mine, axis=1) - is_mine
    matches = jnp.logical_and(
        is_mine[:, :, None] == 1,
        before[:, :, None] == jnp.arange(capacity, dtype=jnp.int32)[None, None, :],
    ).astype(jnp.int32)
    present = jnp.sum(matches, axis=1)
    local_target = jnp.sum(matches * (target_table % TGT_DEV)[:, :, None], axis=1)
    member = (
        jnp.logical_and(
            local_target[None] == jnp.arange(TGT_DEV, dtype=jnp.int32)[:, None, None],
            present[None] == 1,
        )
        .astype(jnp.float32)
        .reshape(TGT_DEV, owners * capacity)
    )
    outgoing = (packed(exposure_flux), packed(exposure_ivar), packed(exposure_res))
    got_flux, got_ivar, got_res = (
        lax.all_to_all(outgoing[0], "tgt", split_axis=0, concat_axis=0, tiled=True),
        lax.all_to_all(outgoing[1], "tgt", split_axis=0, concat_axis=0, tiled=True),
        lax.all_to_all(outgoing[2], "tgt", split_axis=0, concat_axis=0, tiled=True),
    )
    flag_table = valid_of_row.reshape(owners, row_count)
    usable = jnp.sum(matches * flag_table[:, :, None], axis=1)
    weight = got_ivar.astype(jnp.float32) * usable[:, :, None].astype(jnp.float32)
    flux_terms = weight * got_flux.astype(jnp.float32)
    res_terms = (weight[:, :, None, :] * got_res.astype(jnp.float32)).reshape(owners * capacity, -1)
    weight_sum = jnp.dot(
        member, weight.reshape(owners * capacity, wave_dev), precision=lax.Precision.HIGHEST
    )
    flux_sum = jnp.dot(
        member, flux_terms.reshape(owners * capacity, wave_dev), precision=lax.Precision.HIGHEST
    )
    res_sum = jnp.dot(member, res_terms, precision=lax.Precision.HIGHEST).reshape(
        TGT_DEV, NDIAG, wave_dev
    )
    coadd_flux = flux_sum / weight_sum
    coadd_res = (res_sum / weight_sum[:, None, :]).astype(jnp.bfloat16)
    band_index = lax.axis_index("band")
    weight_all, flux_all = (
        lax.all_gather(weight_sum.astype(jnp.bfloat16), "band", axis=1, tiled=True).astype(
            weight_sum.dtype
        ),
        lax.all_gather(flux_sum.astype(jnp.bfloat16), "band", axis=1, tiled=True).astype(
            flux_sum.dtype
        ),
    )
    shifts = lax.dynamic_slice_in_dim(redshift_shift, band_index * Z_DEV, Z_DEV)
    matrix, right_side = blocked_normals(
        weight_all, flux_all, rest_basis, shifts, 0, weight_all.shape[1]
    )
    fit_gain = fit_from(matrix, right_side)
    return (coadd_flux, coadd_res, fit_gain)

def as_bf16_parts(values, count):
    parts = []
    rest = values
    for step in range(count):
        part = rest.astype(jnp.bfloat16)
        parts.append(part)
        rest = rest - part.astype(jnp.float32)
    return parts


def exact_dot(left, right, dims, count):
    total = None
    for part in as_bf16_parts(left, count):
        term = lax.dot_general(part, right, (dims, ((), ())), preferred_element_type=jnp.float32)
        total = term if total is None else total + term
    return total


def partial_kernel(
    target_s, valid_s, shift_s, target_v, valid_v, ivar, flux, res, basis,
    wf_out, res_out, win_out, weight, totals, packed, rest16,
):
    owners = target_v.shape[0]
    rows = ivar.shape[0]
    pieces = res_out.shape[0]
    lanes = res_out.shape[-1]
    waves = win_out.shape[2]
    device = lax.axis_index("tgt")
    first_row = device * rows
    ivar_all = ivar[...]
    weight[...] = ivar_all.astype(jnp.float32)
    totals[...] = jnp.zeros_like(totals)

    def add_row(r, carry):
        target = target_s[first_row + r]
        flag = valid_s[first_row + r].astype(jnp.float32)
        row = weight[pl.ds(r, 1), :] * flag
        totals[target] = totals[target] + row * res[r].astype(jnp.float32)
        return carry

    lax.fori_loop(0, rows, add_row, 0, unroll=4)

    own_target = target_v[pl.ds(device, 1), :]
    own_valid = valid_v[pl.ds(device, 1), :]
    ids = lax.broadcasted_iota(jnp.int32, (owners * TGT_DEV, rows), 0)
    member = jnp.where(ids == own_target, own_valid, 0).astype(jnp.float32).astype(jnp.bfloat16)
    dims = ((1,), (0,))
    weight_part = lax.dot_general(
        member, ivar_all, (dims, ((), ())), preferred_element_type=jnp.float32
    )
    product = weight[...] * flux[...].astype(jnp.float32)
    flux_part = None
    for part in as_bf16_parts(product, 2):
        term = lax.dot_general(member, part, (dims, ((), ())), preferred_element_type=jnp.float32)
        flux_part = term if flux_part is None else flux_part + term
    for o in range(owners):
        span = slice(o * TGT_DEV, (o + 1) * TGT_DEV)
        wf_out[o % 2, o // 2, 0:TGT_DEV, :] = weight_part[span].astype(jnp.bfloat16)
        wf_out[o % 2, o // 2, TGT_DEV:, :] = flux_part[span].astype(jnp.bfloat16)

    def pack_owner(o, carry):
        for t in range(TGT_DEV):
            packed[t * NDIAG : (t + 1) * NDIAG, :] = totals[o * TGT_DEV + t]
        for p in range(pieces):
            res_out[p, o % 2, o // 2] = packed[:, p * lanes : (p + 1) * lanes].astype(jnp.bfloat16)
        return carry

    lax.fori_loop(0, owners, pack_owner, 0)

    basis_count = basis.shape[0]
    rest16[...] = jnp.zeros_like(rest16)
    rest16[0:basis_count, :] = basis[...]
    band = lax.axis_index("band")
    for z in range(Z_DEV):
        shift = shift_s[band * Z_DEV + z]
        start = pl.multiple_of((shift // 128) * 128, 128)
        wide = rest16[:, pl.ds(start, waves + 128)]
        moved = pltpu.roll(wide, (waves + 128) - shift % 128, 1)
        for b in range(basis_count):
            win_out[b, z : z + 1, :] = moved[b : b + 1, 0:waves]


def exchange_kernel(
    wf, res, win, flux_out, res_out, gain_out,
    wf_x, res_x, wf_to, res_to, wf_z, res_z, wf_own, res_own, band_own, band_in,
    normal, right, final, inverse,
    x_send, x_recv, z_send, z_recv, b_send, b_recv,
):
    pieces = res.shape[0]
    high_count = res.shape[2]
    lanes = res.shape[-1]
    bands = lax.axis_size("band")
    owners = lax.axis_size("tgt")
    wave_dev = wf.shape[-1]
    device = lax.axis_index("tgt")
    band = lax.axis_index("band")
    high = device // 2
    low = device % 2
    partner = high * 2 + (1 - low)

    def peer(d):
        return lax.rem(high + d, high_count) * 2 + low

    def band_peer(d):
        return lax.rem(band + d, bands)

    barrier = pltpu.get_barrier_semaphore()
    near = [(partner, band)]
    near += [(peer(d), band) for d in range(1, high_count)]
    near += [(device, band_peer(d)) for d in range(1, bands)]
    for place in near:
        pl.semaphore_signal(barrier, inc=1, device_id=place, device_id_type=MESH)
    pl.semaphore_wait(barrier, len(near))

    def copy(source, target, send, recv, place):
        return pltpu.make_async_remote_copy(
            src_ref=source, dst_ref=target, send_sem=send, recv_sem=recv,
            device_id=place, device_id_type=MESH,
        )

    x_copies = [copy(wf.at[1 - low], wf_x, x_send.at[0], x_recv.at[0], (partner, band))]
    for p in range(pieces):
        x_copies.append(
            copy(res.at[p, 1 - low], res_x.at[p], x_send.at[p + 1], x_recv.at[p + 1], (partner, band))
        )
    z_copies = []
    for p in range(pieces + 1):
        row = []
        for d in range(1, high_count):
            source = wf_to.at[d - 1] if p == 0 else res_to.at[p - 1, d - 1]
            target = wf_z.at[d - 1] if p == 0 else res_z.at[p - 1, d - 1]
            row.append(
                copy(source, target, z_send.at[p, d - 1], z_recv.at[p, d - 1], (peer(d), band))
            )
        z_copies.append(row)
    b_copies = [
        copy(band_own, band_in.at[d - 1], b_send.at[d - 1], b_recv.at[d - 1], (device, band_peer(d)))
        for d in range(1, bands)
    ]

    def relay(p):
        x_copies[p].wait_recv()
        if p + AHEAD < len(x_copies):
            x_copies[p + AHEAD].start()
        for d in range(1, high_count):
            h = lax.rem(high + d, high_count)
            if p == 0:
                total = wf[low, h].astype(jnp.float32) + wf_x[h].astype(jnp.float32)
                wf_to[d - 1] = total.astype(jnp.bfloat16)
            else:
                total = res[p - 1, low, h].astype(jnp.float32) + res_x[p - 1, h].astype(jnp.float32)
                res_to[p - 1, d - 1] = total.astype(jnp.bfloat16)
            z_copies[p][d - 1].start()
        if p == 0:
            wf_own[...] = wf[low, high].astype(jnp.float32) + wf_x[high].astype(jnp.float32)
        else:
            res_own[p - 1] = (
                res[p - 1, low, high].astype(jnp.float32) + res_x[p - 1, high].astype(jnp.float32)
            )

    def finish_sums():
        total = wf_own[...]
        for d in range(1, high_count):
            z_copies[0][d - 1].wait_recv()
            total = total + wf_z[d - 1].astype(jnp.float32)
        band_own[...] = total.astype(jnp.bfloat16)
        for step in b_copies:
            step.start()
        weight_sum = total[0:TGT_DEV]
        flux_out[...] = total[TGT_DEV:] / weight_sum
        inverse[...] = 1.0 / weight_sum

    def fit_block(d):
        if d == 0:
            source, place = band_own, band
        else:
            b_copies[d - 1].wait_recv()
            source, place = band_in.at[d - 1], lax.rem(band + (bands - d), bands)
        dims = ((1,), (1,))
        for step in range(wave_dev // FIT_LANES):
            span = slice(step * FIT_LANES, (step + 1) * FIT_LANES)
            at = pl.multiple_of(place * wave_dev + step * FIT_LANES, FIT_LANES)
            waves = [win[b, :, pl.ds(at, FIT_LANES)] for b in range(win.shape[0])]
            pairs = [waves[int(b)] * waves[int(c)] for b, c in zip(pair_first, pair_second)]
            pairs.append(pairs[0])
            matrix = exact_dot(jnp.concatenate(pairs, axis=0), source[0:TGT_DEV, span], dims, 3)
            sides = exact_dot(jnp.concatenate(waves, axis=0), source[TGT_DEV:, span], dims, 3)
            if d == 0 and step == 0:
                normal[...] = matrix
                right[...] = sides
            else:
                normal[...] += matrix
                right[...] += sides

    def solve():
        matrix = [normal[Z_DEV * p : Z_DEV * (p + 1), :] for p in range(len(pair_first))]
        sides = [right[Z_DEV * b : Z_DEV * (b + 1), :] for b in range(win.shape[0])]
        gain_out[...] = solve_normal(matrix, jnp.stack(sides))

    def finish_piece(p):
        total = res_own[p]
        for d in range(1, high_count):
            z_copies[p + 1][d - 1].wait_recv()
            total = total + res_z[p, d - 1].astype(jnp.float32)
        final[...] = total
        span = slice(p * lanes, (p + 1) * lanes)
        for t in range(TGT_DEV):
            one = final[t * NDIAG : (t + 1) * NDIAG, :] * inverse[t : t + 1, span]
            res_out[t, :, span] = one.astype(jnp.bfloat16)

    for p in range(min(AHEAD, len(x_copies))):
        x_copies[p].start()
    jobs = [finish_sums] + [functools.partial(fit_block, d) for d in range(bands)] + [solve]
    relay(0)
    finished = 0
    for p in range(1, pieces + 1):
        relay(p)
        if jobs:
            jobs.pop(0)()
        if p >= 4:
            finish_piece(finished)
            finished += 1
    while jobs:
        jobs.pop(0)()
    while finished < pieces:
        finish_piece(finished)
        finished += 1
    for step in x_copies + b_copies + [step for row in z_copies for step in row]:
        step.wait_send()


def dense_shards(
    exposure_flux, exposure_ivar, exposure_res, target_of_row, valid_of_row, rest_basis, redshift_shift
):
    owners = lax.axis_size("tgt")
    bands = lax.axis_size("band")
    rows, wave_dev = exposure_flux.shape
    waves = wave_dev * bands
    basis_count = rest_basis.shape[0]
    high_count = owners // 2
    pieces = wave_dev // PIECE_LANES
    packed_rows = TGT_DEV * NDIAG
    pair_rows = Z_DEV * (len(pair_first) + 1)
    vmem = pl.BlockSpec(memory_space=pltpu.VMEM)
    smem = pl.BlockSpec(memory_space=pltpu.SMEM)
    half, full = jnp.bfloat16, jnp.float32
    wf, res, win = pl.pallas_call(
        partial_kernel,
        out_shape=(
            jax.ShapeDtypeStruct((2, high_count, 2 * TGT_DEV, wave_dev), half),
            jax.ShapeDtypeStruct((pieces, 2, high_count, packed_rows, PIECE_LANES), half),
            jax.ShapeDtypeStruct((basis_count, Z_DEV, waves), full),
        ),
        in_specs=[smem] * 3 + [vmem] * 6,
        out_specs=(vmem, vmem, vmem),
        scratch_shapes=[
            pltpu.VMEM((rows, wave_dev), full),
            pltpu.VMEM((owners * TGT_DEV, NDIAG, wave_dev), full),
            pltpu.VMEM((packed_rows, wave_dev), full),
            pltpu.VMEM((16, rest_basis.shape[1]), full),
        ],
        compiler_params=pltpu.CompilerParams(vmem_limit_bytes=VMEM_LIMIT),
        name="partial_sums",
    )(
        target_of_row, valid_of_row, redshift_shift,
        target_of_row.reshape(owners, rows), valid_of_row.reshape(owners, rows),
        exposure_ivar, exposure_flux, exposure_res, rest_basis,
    )
    peers = high_count - 1
    block = (packed_rows, PIECE_LANES)
    sums = (2 * TGT_DEV, wave_dev)
    dma = pltpu.SemaphoreType.DMA
    coadd_flux, coadd_res, gain = pl.pallas_call(
        exchange_kernel,
        out_shape=(
            jax.ShapeDtypeStruct((TGT_DEV, wave_dev), full),
            jax.ShapeDtypeStruct((TGT_DEV, NDIAG, wave_dev), half),
            jax.ShapeDtypeStruct((Z_DEV, TGT_DEV), full),
        ),
        in_specs=[vmem] * 3,
        out_specs=(vmem, vmem, vmem),
        scratch_shapes=[
            pltpu.VMEM((high_count,) + sums, half),
            pltpu.VMEM((pieces, high_count) + block, half),
            pltpu.VMEM((peers,) + sums, half),
            pltpu.VMEM((pieces, peers) + block, half),
            pltpu.VMEM((peers,) + sums, half),
            pltpu.VMEM((pieces, peers) + block, half),
            pltpu.VMEM(sums, full),
            pltpu.VMEM((pieces,) + block, full),
            pltpu.VMEM(sums, half),
            pltpu.VMEM((bands - 1,) + sums, half),
            pltpu.VMEM((pair_rows, TGT_DEV), full),
            pltpu.VMEM((Z_DEV * basis_count, TGT_DEV), full),
            pltpu.VMEM(block, full),
            pltpu.VMEM((TGT_DEV, wave_dev), full),
            dma((pieces + 1,)),
            dma((pieces + 1,)),
            dma((pieces + 1, peers)),
            dma((pieces + 1, peers)),
            dma((bands - 1,)),
            dma((bands - 1,)),
        ],
        compiler_params=pltpu.CompilerParams(
            vmem_limit_bytes=VMEM_LIMIT, collective_id=0, has_side_effects=True
        ),
        name="exchange_and_fit",
    )(wf, res, win)
    return (coadd_flux, coadd_res, gain.T)


def solution(mesh):
    in_specs = (P("tgt", "band"), P("tgt", "band"), P("tgt", None, "band"), P(), P(), P(), P())
    out_specs = (P("tgt", "band"), P("tgt", None, "band"), P("tgt", "band"))
    owners = mesh.shape["tgt"]

    def whole(*args):
        rows = args[0].shape[0] // owners
        body = dense_shards if owners * TGT_DEV <= 2 * rows and owners % 2 == 0 else shards
        return jax.shard_map(
            body, mesh=mesh, in_specs=in_specs, out_specs=out_specs, check_vma=False
        )(*args)

    return whole
```

```python
import functools

import jax
import jax.numpy as jnp
import numpy as np
from jax import lax
from jax.experimental import pallas as pl
from jax.experimental.pallas import tpu as pltpu
from jax.sharding import PartitionSpec as P

TGT_DEV = 16
NDIAG = 11
Z_DEV = 8
FIT_LANES = 256
AHEAD = 3
VMEM_LIMIT = 60 * 1024 * 1024
MESH = pl.DeviceIdType.MESH


pair_first, pair_second = np.triu_indices(10)


def solve_normal(matrix, right_side):
    basis_count = right_side.shape[0]
    rows_of = [[None] * basis_count for column in range(basis_count)]
    for p in range(len(pair_first)):
        b = int(pair_first[p])
        c = int(pair_second[p])
        rows_of[b][c] = matrix[p]
        rows_of[c][b] = matrix[p]
    vector = [right_side[b] for b in range(basis_count)]
    for k in range(basis_count):
        inverse = 1.0 / rows_of[k][k]
        for r in range(k + 1, basis_count):
            factor = rows_of[r][k] * inverse
            for c in range(k + 1, basis_count):
                rows_of[r][c] = rows_of[r][c] - factor * rows_of[k][c]
            vector[r] = vector[r] - factor * vector[k]
    answer = [None] * basis_count
    for k in reversed(range(basis_count)):
        running = vector[k]
        for c in range(k + 1, basis_count):
            running = running - rows_of[k][c] * answer[c]
        answer[k] = running / rows_of[k][k]
    gain_total = right_side[0] * answer[0]
    for b in range(1, basis_count):
        gain_total = gain_total + right_side[b] * answer[b]
    return gain_total


def basis_windows(rest_basis, shifts, first_wave, length):

    def one_shift(shift_value):
        return lax.dynamic_slice_in_dim(rest_basis, first_wave + shift_value, length, axis=1)

    return jax.vmap(one_shift)(shifts)


def normal_terms(weight_sum, flux_sum, windows):
    products = windows[:, pair_first, :] * windows[:, pair_second, :]
    matrix = jnp.einsum("ti,zpi->ztp", weight_sum, products, precision=lax.Precision.HIGHEST)
    right_side = jnp.einsum("ti,zbi->ztb", flux_sum, windows, precision=lax.Precision.HIGHEST)
    return (matrix, right_side)


def blocked_normals(weight_sum, flux_sum, rest_basis, shifts, first_wave, length):
    total_shifts = shifts.shape[0]
    block_size = 8
    grouped = shifts.reshape(total_shifts // block_size, block_size)

    def one_block(shift_block):
        return normal_terms(
            weight_sum, flux_sum, basis_windows(rest_basis, shift_block, first_wave, length)
        )

    matrix, right_side = lax.map(one_block, grouped)
    return (
        matrix.reshape((total_shifts,) + matrix.shape[2:]),
        right_side.reshape((total_shifts,) + right_side.shape[2:]),
    )


def fit_from(matrix, right_side):
    pairs = jnp.transpose(matrix, (2, 0, 1)).reshape(matrix.shape[2], -1)
    sides = jnp.transpose(right_side, (2, 0, 1)).reshape(right_side.shape[2], -1)
    gain = solve_normal(pairs, sides).reshape(matrix.shape[0], matrix.shape[1])
    return gain.T


def shards(
    exposure_flux,
    exposure_ivar,
    exposure_res,
    target_of_row,
    valid_of_row,
    rest_basis,
    redshift_shift,
):
    owners = lax.axis_size("tgt")
    device = lax.axis_index("tgt")
    row_count = exposure_flux.shape[0]
    wave_dev = exposure_flux.shape[1]
    capacity = 2 * row_count // owners
    own_target = lax.dynamic_slice_in_dim(target_of_row, device * row_count, row_count)
    owner_of = own_target // TGT_DEV
    row_ids = jnp.arange(row_count, dtype=jnp.int32)
    earlier = row_ids[None, :] < row_ids[:, None]
    position = jnp.sum(jnp.logical_and(owner_of[:, None] == owner_of[None, :], earlier), axis=1)
    slot_index = owner_of * capacity + position
    source_row = jnp.full((owners * capacity,), row_count, jnp.int32).at[slot_index].set(row_ids)

    def packed(values):
        gathered = jnp.take(values, source_row, axis=0, mode="fill", fill_value=0)
        return gathered.reshape((owners, capacity) + values.shape[1:])

    target_table = target_of_row.reshape(owners, row_count)
    is_mine = (target_table // TGT_DEV == device).astype(jnp.int32)
    before = jnp.cumsum(is_mine, axis=1) - is_mine
    matches = jnp.logical_and(
        is_mine[:, :, None] == 1,
        before[:, :, None] == jnp.arange(capacity, dtype=jnp.int32)[None, None, :],
    ).astype(jnp.int32)
    present = jnp.sum(matches, axis=1)
    local_target = jnp.sum(matches * (target_table % TGT_DEV)[:, :, None], axis=1)
    member = (
        jnp.logical_and(
            local_target[None] == jnp.arange(TGT_DEV, dtype=jnp.int32)[:, None, None],
            present[None] == 1,
        )
        .astype(jnp.float32)
        .reshape(TGT_DEV, owners * capacity)
    )
    outgoing = (packed(exposure_flux), packed(exposure_ivar), packed(exposure_res))
    got_flux, got_ivar, got_res = (
        lax.all_to_all(outgoing[0], "tgt", split_axis=0, concat_axis=0, tiled=True),
        lax.all_to_all(outgoing[1], "tgt", split_axis=0, concat_axis=0, tiled=True),
        lax.all_to_all(outgoing[2], "tgt", split_axis=0, concat_axis=0, tiled=True),
    )
    flag_table = valid_of_row.reshape(owners, row_count)
    usable = jnp.sum(matches * flag_table[:, :, None], axis=1)
    weight = got_ivar.astype(jnp.float32) * usable[:, :, None].astype(jnp.float32)
    flux_terms = weight * got_flux.astype(jnp.float32)
    res_terms = (weight[:, :, None, :] * got_res.astype(jnp.float32)).reshape(owners * capacity, -1)
    weight_sum = jnp.dot(
        member, weight.reshape(owners * capacity, wave_dev), precision=lax.Precision.HIGHEST
    )
    flux_sum = jnp.dot(
        member, flux_terms.reshape(owners * capacity, wave_dev), precision=lax.Precision.HIGHEST
    )
    res_sum = jnp.dot(member, res_terms, precision=lax.Precision.HIGHEST).reshape(
        TGT_DEV, NDIAG, wave_dev
    )
    coadd_flux = flux_sum / weight_sum
    coadd_res = (res_sum / weight_sum[:, None, :]).astype(jnp.bfloat16)
    band_index = lax.axis_index("band")
    weight_all, flux_all = (
        lax.all_gather(weight_sum.astype(jnp.bfloat16), "band", axis=1, tiled=True).astype(
            weight_sum.dtype
        ),
        lax.all_gather(flux_sum.astype(jnp.bfloat16), "band", axis=1, tiled=True).astype(
            flux_sum.dtype
        ),
    )
    shifts = lax.dynamic_slice_in_dim(redshift_shift, band_index * Z_DEV, Z_DEV)
    matrix, right_side = blocked_normals(
        weight_all, flux_all, rest_basis, shifts, 0, weight_all.shape[1]
    )
    fit_gain = fit_from(matrix, right_side)
    return (coadd_flux, coadd_res, fit_gain)

def as_bf16_parts(values, count):
    parts = []
    rest = values
    for step in range(count):
        part = rest.astype(jnp.bfloat16)
        parts.append(part)
        rest = rest - part.astype(jnp.float32)
    return parts


def exact_dot(left, right, dims, count):
    total = None
    for part in as_bf16_parts(left, count):
        term = lax.dot_general(part, right, (dims, ((), ())), preferred_element_type=jnp.float32)
        total = term if total is None else total + term
    return total


def fused_kernel(
    shift_s, target_v, valid_v, basis, ivar_any, flux_any, res_any,
    flux_out, res_out, gain_out,
    ivar, flux, res, weight, doubled, win,
    sums_x, sums_in, sums_to, sums_z, sums_own,
    res_x, res_in, res_to, res_z, res_own,
    band_own, band_in, normal, right, inverse,
    l_sem, x_send, x_recv, z_send, z_recv, b_send, b_recv,
):
    owners, rows = target_v.shape
    channels, wave_dev = res.shape[0], res.shape[-1]
    bands = lax.axis_size("band")
    high_count = owners // 2
    waves = win.shape[2]
    basis_count = basis.shape[0]
    device = lax.axis_index("tgt")
    band = lax.axis_index("band")
    high = device // 2
    low = device % 2
    partner = high * 2 + (1 - low)

    def peer(d):
        return lax.rem(high + d, high_count) * 2 + low

    def band_peer(d):
        return lax.rem(band + d, bands)

    loads = [
        pltpu.make_async_copy(ivar_any, ivar, l_sem.at[0]),
        pltpu.make_async_copy(flux_any, flux, l_sem.at[1]),
    ]
    for k in range(channels):
        loads.append(pltpu.make_async_copy(res_any.at[k], res.at[k], l_sem.at[k + 2]))
    for step in loads:
        step.start()

    barrier = pltpu.get_barrier_semaphore()
    near = [(partner, band)]
    near += [(peer(d), band) for d in range(1, high_count)]
    near += [(device, band_peer(d)) for d in range(1, bands)]
    for place in near:
        pl.semaphore_signal(barrier, inc=1, device_id=place, device_id_type=MESH)

    def copy(source, target, send, recv, place):
        return pltpu.make_async_remote_copy(
            src_ref=source, dst_ref=target, send_sem=send, recv_sem=recv,
            device_id=place, device_id_type=MESH,
        )

    x_copies = [copy(sums_x, sums_in, x_send.at[0], x_recv.at[0], (partner, band))]
    for k in range(channels):
        x_copies.append(
            copy(res_x.at[k], res_in.at[k], x_send.at[k + 1], x_recv.at[k + 1], (partner, band))
        )
    z_copies = []
    for p in range(channels + 1):
        row = []
        for d in range(1, high_count):
            source = sums_to.at[d - 1] if p == 0 else res_to.at[p - 1, d - 1]
            target = sums_z.at[d - 1] if p == 0 else res_z.at[p - 1, d - 1]
            row.append(
                copy(source, target, z_send.at[p, d - 1], z_recv.at[p, d - 1], (peer(d), band))
            )
        z_copies.append(row)
    b_copies = [
        copy(band_own, band_in.at[d - 1], b_send.at[d - 1], b_recv.at[d - 1], (device, band_peer(d)))
        for d in range(1, bands)
    ]

    count = owners * TGT_DEV
    half = count // 2
    ids = lax.broadcasted_iota(jnp.int32, (count, rows), 0)
    own_half = (ids >= half).astype(jnp.int32)
    distance = (ids - own_half * half) // TGT_DEV
    row_low = own_half * low + (1 - own_half) * (1 - low)
    row_target = (lax.rem(distance + high, high_count) * 2 + row_low) * TGT_DEV + ids % TGT_DEV
    own_target = target_v[pl.ds(device, 1), :]
    own_valid = valid_v[pl.ds(device, 1), :]
    member = jnp.where(row_target == own_target, own_valid, 0).astype(jnp.float32)
    member = member.astype(jnp.bfloat16)
    doubled[...] = jnp.concatenate([member, member], axis=1)
    dims = (((1,), (0,)), ((), ()))

    def summed(values):
        product = weight[...] * values.astype(jnp.float32)
        parts = jnp.concatenate(as_bf16_parts(product, 2), axis=0)
        return lax.dot_general(doubled[...], parts, dims, preferred_element_type=jnp.float32)

    def prepare_sums():
        loads[0].wait()
        loads[1].wait()
        weight[...] = ivar[...].astype(jnp.float32)
        for place, part in (
            (0, lax.dot_general(member, ivar[...], dims, preferred_element_type=jnp.float32)),
            (TGT_DEV, summed(flux[...])),
        ):
            for d in range(high_count):
                span = slice(d * TGT_DEV, (d + 1) * TGT_DEV)
                other = slice(half + d * TGT_DEV, half + (d + 1) * TGT_DEV)
                sums_x[d, place : place + TGT_DEV, :] = part[span].astype(jnp.bfloat16)
                sums_own[d, place : place + TGT_DEV, :] = part[other]

    def prepare(k):
        loads[k + 2].wait()
        part = summed(res[k])
        for d in range(high_count):
            span = slice(d * TGT_DEV, (d + 1) * TGT_DEV)
            other = slice(half + d * TGT_DEV, half + (d + 1) * TGT_DEV)
            res_x[k, d] = part[span].astype(jnp.bfloat16)
            res_own[k, d] = part[other]

    def relay(p):
        x_copies[p].wait_recv()
        if p + AHEAD <= channels:
            prepare(p + AHEAD - 1)
            x_copies[p + AHEAD].start()
        for d in range(1, high_count):
            if p == 0:
                total = sums_own[d] + sums_in[d].astype(jnp.float32)
                sums_to[d - 1] = total.astype(jnp.bfloat16)
            else:
                total = res_own[p - 1, d] + res_in[p - 1, d].astype(jnp.float32)
                res_to[p - 1, d - 1] = total.astype(jnp.bfloat16)
            z_copies[p][d - 1].start()

    def finish_sums():
        total = sums_own[0] + sums_in[0].astype(jnp.float32)
        for d in range(1, high_count):
            z_copies[0][d - 1].wait_recv()
            total = total + sums_z[d - 1].astype(jnp.float32)
        band_own[...] = total.astype(jnp.bfloat16)
        for step in b_copies:
            step.start()
        weight_sum = total[0:TGT_DEV]
        flux_out[...] = total[TGT_DEV:] / weight_sum
        inverse[...] = 1.0 / weight_sum

    def make_windows(first, last):
        ids8 = lax.broadcasted_iota(jnp.int32, (Z_DEV, 128), 0)
        shift = jnp.zeros((Z_DEV, 128), jnp.int32)
        for z in range(Z_DEV):
            shift = jnp.where(ids8 == z, shift_s[band * Z_DEV + z], shift)
        spare = basis.shape[1] - waves

        def one_basis(b, carry):
            rows_of = jnp.broadcast_to(basis[pl.ds(b, 1), :], (Z_DEV, basis.shape[1]))
            step = spare // 2
            while step >= 1:
                if step >= 128:
                    width = rows_of.shape[1] - step
                    moved, kept = rows_of[:, step:], rows_of[:, :width]
                else:
                    width = rows_of.shape[1]
                    moved, kept = pltpu.roll(rows_of, width - step, 1), rows_of
                wide = jnp.concatenate([shift] * (width // 128), axis=1)
                rows_of = jnp.where((wide & step) != 0, moved, kept)
                step //= 2
            win[b] = rows_of[:, :waves]
            return carry

        lax.fori_loop(first, last, one_basis, 0)

    def fit_block(d):
        if d == 0:
            source, place = band_own, band
        else:
            b_copies[d - 1].wait_recv()
            source, place = band_in.at[d - 1], lax.rem(band + (bands - d), bands)
        last = ((1,), (1,))
        for step in range(wave_dev // FIT_LANES):
            span = slice(step * FIT_LANES, (step + 1) * FIT_LANES)
            at = pl.multiple_of(place * wave_dev + step * FIT_LANES, FIT_LANES)
            bases = [win[b, :, pl.ds(at, FIT_LANES)] for b in range(basis_count)]
            pairs = [bases[int(b)] * bases[int(c)] for b, c in zip(pair_first, pair_second)]
            pairs.append(pairs[0])
            matrix = exact_dot(jnp.concatenate(pairs, axis=0), source[0:TGT_DEV, span], last, 3)
            sides = exact_dot(jnp.concatenate(bases, axis=0), source[TGT_DEV:, span], last, 3)
            if d == 0 and step == 0:
                normal[...] = matrix
                right[...] = sides
            else:
                normal[...] += matrix
                right[...] += sides

    def solve():
        matrix = [normal[Z_DEV * p : Z_DEV * (p + 1), :] for p in range(len(pair_first))]
        sides = [right[Z_DEV * b : Z_DEV * (b + 1), :] for b in range(basis_count)]
        gain_out[...] = solve_normal(matrix, jnp.stack(sides))

    def finish(k):
        total = res_own[k, 0] + res_in[k, 0].astype(jnp.float32)
        for d in range(1, high_count):
            z_copies[k + 1][d - 1].wait_recv()
            total = total + res_z[k, d - 1].astype(jnp.float32)
        res_out[k] = (total * inverse[...]).astype(jnp.bfloat16)

    prepare_sums()
    pl.semaphore_wait(barrier, len(near))
    x_copies[0].start()
    for p in range(1, AHEAD):
        prepare(p - 1)
        x_copies[p].start()
    jobs = [functools.partial(make_windows, 0, basis_count // 2)]
    jobs += [functools.partial(make_windows, basis_count // 2, basis_count), finish_sums]
    jobs += [functools.partial(fit_block, d) for d in range(bands)] + [solve]
    relay(0)
    finished = 0
    for p in range(1, channels + 1):
        relay(p)
        if jobs:
            jobs.pop(0)()
        if p >= 6:
            finish(finished)
            finished += 1
    while jobs:
        jobs.pop(0)()
    while finished < channels:
        finish(finished)
        finished += 1
    for step in x_copies + b_copies + [step for row in z_copies for step in row]:
        step.wait_send()


def dense_shards(
    exposure_flux, exposure_ivar, exposure_res, target_of_row, valid_of_row, rest_basis, redshift_shift
):
    owners = lax.axis_size("tgt")
    bands = lax.axis_size("band")
    rows, wave_dev = exposure_flux.shape
    waves = wave_dev * bands
    basis_count = rest_basis.shape[0]
    high_count = owners // 2
    peers = high_count - 1
    pair_rows = Z_DEV * (len(pair_first) + 1)
    vmem = pl.BlockSpec(memory_space=pltpu.VMEM)
    smem = pl.BlockSpec(memory_space=pltpu.SMEM)
    hbm = pl.BlockSpec(memory_space=pl.ANY)
    half, full = jnp.bfloat16, jnp.float32
    block = (TGT_DEV, wave_dev)
    sums = (2 * TGT_DEV, wave_dev)
    dma = pltpu.SemaphoreType.DMA
    coadd_flux, coadd_res, gain = pl.pallas_call(
        fused_kernel,
        out_shape=(
            jax.ShapeDtypeStruct(block, full),
            jax.ShapeDtypeStruct((NDIAG,) + block, half),
            jax.ShapeDtypeStruct((Z_DEV, TGT_DEV), full),
        ),
        in_specs=[smem, vmem, vmem, vmem, hbm, hbm, hbm],
        out_specs=(vmem, vmem, vmem),
        scratch_shapes=[
            pltpu.VMEM((rows, wave_dev), half),
            pltpu.VMEM((rows, wave_dev), half),
            pltpu.VMEM((NDIAG, rows, wave_dev), half),
            pltpu.VMEM((rows, wave_dev), full),
            pltpu.VMEM((owners * TGT_DEV, 2 * rows), half),
            pltpu.VMEM((basis_count, Z_DEV, waves), full),
            pltpu.VMEM((high_count,) + sums, half),
            pltpu.VMEM((high_count,) + sums, half),
            pltpu.VMEM((peers,) + sums, half),
            pltpu.VMEM((peers,) + sums, half),
            pltpu.VMEM((high_count,) + sums, full),
            pltpu.VMEM((NDIAG, high_count) + block, half),
            pltpu.VMEM((NDIAG, high_count) + block, half),
            pltpu.VMEM((NDIAG, peers) + block, half),
            pltpu.VMEM((NDIAG, peers) + block, half),
            pltpu.VMEM((NDIAG, high_count) + block, full),
            pltpu.VMEM(sums, half),
            pltpu.VMEM((bands - 1,) + sums, half),
            pltpu.VMEM((pair_rows, TGT_DEV), full),
            pltpu.VMEM((Z_DEV * basis_count, TGT_DEV), full),
            pltpu.VMEM(block, full),
            dma((NDIAG + 2,)),
            dma((NDIAG + 1,)),
            dma((NDIAG + 1,)),
            dma((NDIAG + 1, peers)),
            dma((NDIAG + 1, peers)),
            dma((bands - 1,)),
            dma((bands - 1,)),
        ],
        compiler_params=pltpu.CompilerParams(
            vmem_limit_bytes=VMEM_LIMIT, collective_id=0, has_side_effects=True
        ),
        name="coadd_and_fit",
    )(
        redshift_shift,
        target_of_row.reshape(owners, rows), valid_of_row.reshape(owners, rows), rest_basis,
        exposure_ivar, exposure_flux, jnp.transpose(exposure_res, (1, 0, 2)),
    )
    return (coadd_flux, jnp.transpose(coadd_res, (1, 0, 2)), gain.T)


def solution(mesh):
    in_specs = (P("tgt", "band"), P("tgt", "band"), P("tgt", None, "band"), P(), P(), P(), P())
    out_specs = (P("tgt", "band"), P("tgt", None, "band"), P("tgt", "band"))
    owners = mesh.shape["tgt"]

    def whole(*args):
        rows = args[0].shape[0] // owners
        body = dense_shards if owners * TGT_DEV <= 2 * rows and owners % 2 == 0 else shards
        return jax.shard_map(
            body, mesh=mesh, in_specs=in_specs, out_specs=out_specs, check_vma=False
        )(*args)

    return whole
```

```python
import functools

import jax
import jax.numpy as jnp
import numpy as np
from jax import lax
from jax.experimental import pallas as pl
from jax.experimental.pallas import tpu as pltpu
from jax.sharding import PartitionSpec as P

TGT_DEV = 16
NDIAG = 11
Z_DEV = 8
FIT_LANES = 256
AHEAD = 4
ORDERS = ((0, 1, 2), (1, 0, 2))
Z_FIRST = (1, 5, 9)
VMEM_LIMIT = 52 * 1024 * 1024
MESH = pl.DeviceIdType.MESH


pair_first, pair_second = np.triu_indices(10)


def solve_normal(matrix, right_side):
    basis_count = right_side.shape[0]
    rows_of = [[None] * basis_count for column in range(basis_count)]
    for p in range(len(pair_first)):
        b = int(pair_first[p])
        c = int(pair_second[p])
        rows_of[b][c] = matrix[p]
        rows_of[c][b] = matrix[p]
    vector = [right_side[b] for b in range(basis_count)]
    for k in range(basis_count):
        inverse = 1.0 / rows_of[k][k]
        for r in range(k + 1, basis_count):
            factor = rows_of[r][k] * inverse
            for c in range(k + 1, basis_count):
                rows_of[r][c] = rows_of[r][c] - factor * rows_of[k][c]
            vector[r] = vector[r] - factor * vector[k]
    answer = [None] * basis_count
    for k in reversed(range(basis_count)):
        running = vector[k]
        for c in range(k + 1, basis_count):
            running = running - rows_of[k][c] * answer[c]
        answer[k] = running / rows_of[k][k]
    gain_total = right_side[0] * answer[0]
    for b in range(1, basis_count):
        gain_total = gain_total + right_side[b] * answer[b]
    return gain_total


def basis_windows(rest_basis, shifts, first_wave, length):

    def one_shift(shift_value):
        return lax.dynamic_slice_in_dim(rest_basis, first_wave + shift_value, length, axis=1)

    return jax.vmap(one_shift)(shifts)


def normal_terms(weight_sum, flux_sum, windows):
    products = windows[:, pair_first, :] * windows[:, pair_second, :]
    matrix = jnp.einsum("ti,zpi->ztp", weight_sum, products, precision=lax.Precision.HIGHEST)
    right_side = jnp.einsum("ti,zbi->ztb", flux_sum, windows, precision=lax.Precision.HIGHEST)
    return (matrix, right_side)


def blocked_normals(weight_sum, flux_sum, rest_basis, shifts, first_wave, length):
    total_shifts = shifts.shape[0]
    block_size = 8
    grouped = shifts.reshape(total_shifts // block_size, block_size)

    def one_block(shift_block):
        return normal_terms(
            weight_sum, flux_sum, basis_windows(rest_basis, shift_block, first_wave, length)
        )

    matrix, right_side = lax.map(one_block, grouped)
    return (
        matrix.reshape((total_shifts,) + matrix.shape[2:]),
        right_side.reshape((total_shifts,) + right_side.shape[2:]),
    )


def fit_from(matrix, right_side):
    pairs = jnp.transpose(matrix, (2, 0, 1)).reshape(matrix.shape[2], -1)
    sides = jnp.transpose(right_side, (2, 0, 1)).reshape(right_side.shape[2], -1)
    gain = solve_normal(pairs, sides).reshape(matrix.shape[0], matrix.shape[1])
    return gain.T


def shards(
    exposure_flux,
    exposure_ivar,
    exposure_res,
    target_of_row,
    valid_of_row,
    rest_basis,
    redshift_shift,
):
    owners = lax.axis_size("tgt")
    device = lax.axis_index("tgt")
    row_count = exposure_flux.shape[0]
    wave_dev = exposure_flux.shape[1]
    capacity = 2 * row_count // owners
    own_target = lax.dynamic_slice_in_dim(target_of_row, device * row_count, row_count)
    owner_of = own_target // TGT_DEV
    row_ids = jnp.arange(row_count, dtype=jnp.int32)
    earlier = row_ids[None, :] < row_ids[:, None]
    position = jnp.sum(jnp.logical_and(owner_of[:, None] == owner_of[None, :], earlier), axis=1)
    slot_index = owner_of * capacity + position
    source_row = jnp.full((owners * capacity,), row_count, jnp.int32).at[slot_index].set(row_ids)

    def packed(values):
        gathered = jnp.take(values, source_row, axis=0, mode="fill", fill_value=0)
        return gathered.reshape((owners, capacity) + values.shape[1:])

    target_table = target_of_row.reshape(owners, row_count)
    is_mine = (target_table // TGT_DEV == device).astype(jnp.int32)
    before = jnp.cumsum(is_mine, axis=1) - is_mine
    matches = jnp.logical_and(
        is_mine[:, :, None] == 1,
        before[:, :, None] == jnp.arange(capacity, dtype=jnp.int32)[None, None, :],
    ).astype(jnp.int32)
    present = jnp.sum(matches, axis=1)
    local_target = jnp.sum(matches * (target_table % TGT_DEV)[:, :, None], axis=1)
    member = (
        jnp.logical_and(
            local_target[None] == jnp.arange(TGT_DEV, dtype=jnp.int32)[:, None, None],
            present[None] == 1,
        )
        .astype(jnp.float32)
        .reshape(TGT_DEV, owners * capacity)
    )
    outgoing = (packed(exposure_flux), packed(exposure_ivar), packed(exposure_res))
    got_flux, got_ivar, got_res = (
        lax.all_to_all(outgoing[0], "tgt", split_axis=0, concat_axis=0, tiled=True),
        lax.all_to_all(outgoing[1], "tgt", split_axis=0, concat_axis=0, tiled=True),
        lax.all_to_all(outgoing[2], "tgt", split_axis=0, concat_axis=0, tiled=True),
    )
    flag_table = valid_of_row.reshape(owners, row_count)
    usable = jnp.sum(matches * flag_table[:, :, None], axis=1)
    weight = got_ivar.astype(jnp.float32) * usable[:, :, None].astype(jnp.float32)
    flux_terms = weight * got_flux.astype(jnp.float32)
    res_terms = (weight[:, :, None, :] * got_res.astype(jnp.float32)).reshape(owners * capacity, -1)
    weight_sum = jnp.dot(
        member, weight.reshape(owners * capacity, wave_dev), precision=lax.Precision.HIGHEST
    )
    flux_sum = jnp.dot(
        member, flux_terms.reshape(owners * capacity, wave_dev), precision=lax.Precision.HIGHEST
    )
    res_sum = jnp.dot(member, res_terms, precision=lax.Precision.HIGHEST).reshape(
        TGT_DEV, NDIAG, wave_dev
    )
    coadd_flux = flux_sum / weight_sum
    coadd_res = (res_sum / weight_sum[:, None, :]).astype(jnp.bfloat16)
    band_index = lax.axis_index("band")
    weight_all, flux_all = (
        lax.all_gather(weight_sum.astype(jnp.bfloat16), "band", axis=1, tiled=True).astype(
            weight_sum.dtype
        ),
        lax.all_gather(flux_sum.astype(jnp.bfloat16), "band", axis=1, tiled=True).astype(
            flux_sum.dtype
        ),
    )
    shifts = lax.dynamic_slice_in_dim(redshift_shift, band_index * Z_DEV, Z_DEV)
    matrix, right_side = blocked_normals(
        weight_all, flux_all, rest_basis, shifts, 0, weight_all.shape[1]
    )
    fit_gain = fit_from(matrix, right_side)
    return (coadd_flux, coadd_res, fit_gain)

def as_bf16_parts(values, count):
    parts = []
    rest = values
    for step in range(count):
        part = rest.astype(jnp.bfloat16)
        parts.append(part)
        rest = rest - part.astype(jnp.float32)
    return parts


def exact_dot(left, right, dims, count):
    total = None
    for part in as_bf16_parts(left, count):
        term = lax.dot_general(part, right, (dims, ((), ())), preferred_element_type=jnp.float32)
        total = term if total is None else total + term
    return total


def fused_kernel(
    shift_s, target_v, valid_v, basis, ivar_any, flux_any, res_any,
    sums_out, res_out, gain_out,
    ivar, flux, res, weight, member, win,
    to_1, in_1, own_1, to_2, in_2, own_2, to_3, in_3, own_3,
    band_own, band_in, normal, right, inverse,
    l_sem, send_sem, recv_sem, b_send, b_recv,
):
    owners, rows = target_v.shape
    channels, wave_dev = res.shape[0], res.shape[-1]
    pieces = channels + 2
    bands = lax.axis_size("band")
    waves = win.shape[2]
    basis_count = basis.shape[0]
    device = lax.axis_index("tgt")
    band = lax.axis_index("band")
    bits = [lax.rem(device // stride, 2) for stride in (1, 2, 4)]
    partners = [device + (1 - 2 * bit) * stride for bit, stride in zip(bits, (1, 2, 4))]

    def band_peer(d):
        return lax.rem(band + d, bands)

    loads = [
        pltpu.make_async_copy(ivar_any, ivar, l_sem.at[0]),
        pltpu.make_async_copy(flux_any, flux, l_sem.at[1]),
    ]
    for k in range(channels):
        loads.append(pltpu.make_async_copy(res_any.at[k], res.at[k], l_sem.at[k + 2]))
    for step in loads:
        step.start()

    barrier = pltpu.get_barrier_semaphore()
    near = [(partner, band) for partner in partners]
    near += [(device, band_peer(d)) for d in range(1, bands)]
    for place in near:
        pl.semaphore_signal(barrier, inc=1, device_id=place, device_id_type=MESH)

    def copy(source, target, send, recv, place):
        return pltpu.make_async_remote_copy(
            src_ref=source, dst_ref=target, send_sem=send, recv_sem=recv,
            device_id=place, device_id_type=MESH,
        )

    def order_of(p):
        return ORDERS[1] if p in Z_FIRST else ORDERS[0]

    rounds = ((to_1, in_1), (to_2, in_2), (to_3, in_3))
    copies = []
    for p in range(pieces):
        copies.append([
            copy(
                source.at[p], target.at[p], send_sem.at[p, r], recv_sem.at[p, r],
                (partners[order_of(p)[r]], band),
            )
            for r, (source, target) in enumerate(rounds)
        ])
    b_copies = [
        copy(band_own, band_in.at[d - 1], b_send.at[d - 1], b_recv.at[d - 1], (device, band_peer(d)))
        for d in range(1, bands)
    ]

    count = owners * TGT_DEV
    ids = lax.broadcasted_iota(jnp.int32, (count, rows), 0)
    own_target = target_v[pl.ds(device, 1), :]
    own_valid = valid_v[pl.ds(device, 1), :]
    for which, order in enumerate(ORDERS):
        owner = jnp.zeros_like(ids)
        for r in range(3):
            mine = (ids // (count >> (r + 1))) % 2
            bit = mine * bits[order[r]] + (1 - mine) * (1 - bits[order[r]])
            owner = owner + bit * (1 << order[r])
        row_target = owner * TGT_DEV + ids % TGT_DEV
        table = jnp.where(row_target == own_target, own_valid, 0).astype(jnp.float32)
        table = table.astype(jnp.bfloat16)
        member[which] = jnp.concatenate([table, table], axis=1)
    dims = (((1,), (0,)), ((), ()))
    half, quarter, eighth = count // 2, count // 4, count // 8

    def prepare(p):
        loads[p].wait()
        which = 1 if p in Z_FIRST else 0
        if p == 0:
            weight[...] = ivar[...].astype(jnp.float32)
            part = lax.dot_general(
                member[which, :, 0:rows], ivar[...], dims, preferred_element_type=jnp.float32
            )
        else:
            values = flux[...] if p == 1 else res[p - 2]
            product = weight[...] * values.astype(jnp.float32)
            parts = jnp.concatenate(as_bf16_parts(product, 2), axis=0)
            part = lax.dot_general(member[which], parts, dims, preferred_element_type=jnp.float32)
        to_1[p] = part[0:half].astype(jnp.bfloat16)
        own_1[p] = part[half:]

    def round_1(p):
        copies[p][0].wait_recv()
        to_2[p] = (own_1[p, 0:quarter] + in_1[p, 0:quarter].astype(jnp.float32)).astype(jnp.bfloat16)
        copies[p][1].start()
        own_2[p] = own_1[p, quarter:] + in_1[p, quarter:].astype(jnp.float32)

    def round_2(p):
        copies[p][1].wait_recv()
        to_3[p] = (own_2[p, 0:eighth] + in_2[p, 0:eighth].astype(jnp.float32)).astype(jnp.bfloat16)
        copies[p][2].start()
        own_3[p] = own_2[p, eighth:] + in_2[p, eighth:].astype(jnp.float32)

    def round_3(p):
        copies[p][2].wait_recv()
        total = own_3[p] + in_3[p].astype(jnp.float32)
        if p < 2:
            sums_out[p] = total
            band_own[p * TGT_DEV : (p + 1) * TGT_DEV, :] = total.astype(jnp.bfloat16)
            if p == 0:
                inverse[...] = 1.0 / total
        else:
            res_out[p - 2] = (total * inverse[...]).astype(jnp.bfloat16)

    def send_sums():
        for step in b_copies:
            step.start()

    def make_windows(first, last):
        ids8 = lax.broadcasted_iota(jnp.int32, (Z_DEV, 128), 0)
        shift = jnp.zeros((Z_DEV, 128), jnp.int32)
        for z in range(Z_DEV):
            shift = jnp.where(ids8 == z, shift_s[band * Z_DEV + z], shift)
        spare = basis.shape[1] - waves

        def one_basis(b, carry):
            rows_of = jnp.broadcast_to(basis[pl.ds(b, 1), :], (Z_DEV, basis.shape[1]))
            step = spare // 2
            while step >= 1:
                if step >= 128:
                    width = rows_of.shape[1] - step
                    moved, kept = rows_of[:, step:], rows_of[:, :width]
                else:
                    width = rows_of.shape[1]
                    moved, kept = pltpu.roll(rows_of, width - step, 1), rows_of
                wide = jnp.concatenate([shift] * (width // 128), axis=1)
                rows_of = jnp.where((wide & step) != 0, moved, kept)
                step //= 2
            win[b] = rows_of[:, :waves]
            return carry

        lax.fori_loop(first, last, one_basis, 0)

    def fit_block(d):
        if d == 0:
            source, place = band_own, band
        else:
            b_copies[d - 1].wait_recv()
            source, place = band_in.at[d - 1], lax.rem(band + (bands - d), bands)
        last = ((1,), (1,))
        for step in range(wave_dev // FIT_LANES):
            span = slice(step * FIT_LANES, (step + 1) * FIT_LANES)
            at = pl.multiple_of(place * wave_dev + step * FIT_LANES, FIT_LANES)
            bases = [win[b, :, pl.ds(at, FIT_LANES)] for b in range(basis_count)]
            pairs = [bases[int(b)] * bases[int(c)] for b, c in zip(pair_first, pair_second)]
            pairs.append(pairs[0])
            matrix = exact_dot(jnp.concatenate(pairs, axis=0), source[0:TGT_DEV, span], last, 3)
            sides = exact_dot(jnp.concatenate(bases, axis=0), source[TGT_DEV:, span], last, 3)
            if d == 0 and step == 0:
                normal[...] = matrix
                right[...] = sides
            else:
                normal[...] += matrix
                right[...] += sides

    def solve():
        matrix = [normal[Z_DEV * p : Z_DEV * (p + 1), :] for p in range(len(pair_first))]
        sides = [right[Z_DEV * b : Z_DEV * (b + 1), :] for b in range(basis_count)]
        gain_out[...] = solve_normal(matrix, jnp.stack(sides))

    prepare(0)
    prepare(1)
    pl.semaphore_wait(barrier, len(near))
    copies[0][0].start()
    copies[1][0].start()
    for p in range(2, AHEAD):
        prepare(p)
        copies[p][0].start()
    jobs = [functools.partial(make_windows, 0, basis_count // 2)]
    jobs += [functools.partial(make_windows, basis_count // 2, basis_count), send_sums]
    jobs += [functools.partial(fit_block, d) for d in range(bands)] + [solve]
    for p in range(pieces + 3):
        if p < pieces:
            round_1(p)
            if p + AHEAD < pieces:
                prepare(p + AHEAD)
                copies[p + AHEAD][0].start()
        if 1 <= p <= pieces:
            round_2(p - 1)
        if p >= 3:
            round_3(p - 3)
        if p >= 2 and jobs:
            jobs.pop(0)()
    for step in b_copies + [step for piece in copies for step in piece]:
        step.wait_send()


def finish_kernel(sums, res, gain, flux_out, res_out, gain_out):
    flux_out[...] = sums[1] / sums[0]
    res_out[...] = res[...]
    gain_out[...] = gain[...]


def dense_shards(
    exposure_flux, exposure_ivar, exposure_res, target_of_row, valid_of_row, rest_basis, redshift_shift
):
    owners = lax.axis_size("tgt")
    bands = lax.axis_size("band")
    rows, wave_dev = exposure_flux.shape
    waves = wave_dev * bands
    basis_count = rest_basis.shape[0]
    pair_rows = Z_DEV * (len(pair_first) + 1)
    vmem = pl.BlockSpec(memory_space=pltpu.VMEM)
    smem = pl.BlockSpec(memory_space=pltpu.SMEM)
    hbm = pl.BlockSpec(memory_space=pl.ANY)
    half, full = jnp.bfloat16, jnp.float32
    block = (TGT_DEV, wave_dev)
    count = owners * TGT_DEV
    pieces = NDIAG + 2
    buffers = []
    for r in range(3):
        shape = (pieces, count >> (r + 1), wave_dev)
        buffers += [pltpu.VMEM(shape, half), pltpu.VMEM(shape, half), pltpu.VMEM(shape, full)]
    dma = pltpu.SemaphoreType.DMA
    sums, coadd_res, gain = pl.pallas_call(
        fused_kernel,
        out_shape=(
            jax.ShapeDtypeStruct((2,) + block, full),
            jax.ShapeDtypeStruct((NDIAG,) + block, half),
            jax.ShapeDtypeStruct((Z_DEV, TGT_DEV), full),
        ),
        in_specs=[smem, vmem, vmem, vmem, hbm, hbm, hbm],
        out_specs=(vmem, vmem, vmem),
        scratch_shapes=[
            pltpu.VMEM((rows, wave_dev), half),
            pltpu.VMEM((rows, wave_dev), half),
            pltpu.VMEM((NDIAG, rows, wave_dev), half),
            pltpu.VMEM((rows, wave_dev), full),
            pltpu.VMEM((2, count, 2 * rows), half),
            pltpu.VMEM((basis_count, Z_DEV, waves), full),
        ] + buffers + [
            pltpu.VMEM((2 * TGT_DEV, wave_dev), half),
            pltpu.VMEM((bands - 1, 2 * TGT_DEV, wave_dev), half),
            pltpu.VMEM((pair_rows, TGT_DEV), full),
            pltpu.VMEM((Z_DEV * basis_count, TGT_DEV), full),
            pltpu.VMEM(block, full),
            dma((pieces,)),
            dma((pieces, 3)),
            dma((pieces, 3)),
            dma((bands - 1,)),
            dma((bands - 1,)),
        ],
        compiler_params=pltpu.CompilerParams(
            vmem_limit_bytes=VMEM_LIMIT, collective_id=0, has_side_effects=True
        ),
        name="coadd_and_fit",
    )(
        redshift_shift,
        target_of_row.reshape(owners, rows), valid_of_row.reshape(owners, rows), rest_basis,
        exposure_ivar, exposure_flux, jnp.transpose(exposure_res, (1, 0, 2)),
    )
    coadd_flux, coadd_res, gain = pl.pallas_call(
        finish_kernel,
        out_shape=(
            jax.ShapeDtypeStruct(block, full),
            jax.ShapeDtypeStruct(coadd_res.shape, half),
            jax.ShapeDtypeStruct(gain.shape, full),
        ),
        in_specs=[vmem] * 3,
        out_specs=(vmem, vmem, vmem),
        name="finish",
    )(sums, coadd_res, gain)
    return (coadd_flux, jnp.transpose(coadd_res, (1, 0, 2)), gain.T)


def solution(mesh):
    in_specs = (P("tgt", "band"), P("tgt", "band"), P("tgt", None, "band"), P(), P(), P(), P())
    out_specs = (P("tgt", "band"), P("tgt", None, "band"), P("tgt", "band"))
    owners = mesh.shape["tgt"]

    def whole(*args):
        rows = args[0].shape[0] // owners
        body = dense_shards if owners * TGT_DEV <= 2 * rows and owners == 8 else shards
        return jax.shard_map(
            body, mesh=mesh, in_specs=in_specs, out_specs=out_specs, check_vma=False
        )(*args)

    return whole
```

```python
import functools

import jax
import jax.numpy as jnp
import numpy as np
from jax import lax
from jax.experimental import pallas as pl
from jax.experimental.pallas import tpu as pltpu
from jax.sharding import PartitionSpec as P

TGT_DEV = 16
NDIAG = 11
Z_DEV = 8
FIT_LANES = 256
AHEAD = 6
FIT_PARTS = 2
ORDERS = ((0, 1, 2), (1, 0, 2))
Z_FIRST = (1, 5, 9)
VMEM_LIMIT = 60 * 1024 * 1024
MESH = pl.DeviceIdType.MESH


pair_first, pair_second = np.triu_indices(10)


def solve_normal(matrix, right_side):
    basis_count = right_side.shape[0]
    rows_of = [[None] * basis_count for column in range(basis_count)]
    for p in range(len(pair_first)):
        b = int(pair_first[p])
        c = int(pair_second[p])
        rows_of[b][c] = matrix[p]
        rows_of[c][b] = matrix[p]
    vector = [right_side[b] for b in range(basis_count)]
    for k in range(basis_count):
        inverse = 1.0 / rows_of[k][k]
        for r in range(k + 1, basis_count):
            factor = rows_of[r][k] * inverse
            for c in range(k + 1, basis_count):
                rows_of[r][c] = rows_of[r][c] - factor * rows_of[k][c]
            vector[r] = vector[r] - factor * vector[k]
    answer = [None] * basis_count
    for k in reversed(range(basis_count)):
        running = vector[k]
        for c in range(k + 1, basis_count):
            running = running - rows_of[k][c] * answer[c]
        answer[k] = running / rows_of[k][k]
    gain_total = right_side[0] * answer[0]
    for b in range(1, basis_count):
        gain_total = gain_total + right_side[b] * answer[b]
    return gain_total


def basis_windows(rest_basis, shifts, first_wave, length):

    def one_shift(shift_value):
        return lax.dynamic_slice_in_dim(rest_basis, first_wave + shift_value, length, axis=1)

    return jax.vmap(one_shift)(shifts)


def normal_terms(weight_sum, flux_sum, windows):
    products = windows[:, pair_first, :] * windows[:, pair_second, :]
    matrix = jnp.einsum("ti,zpi->ztp", weight_sum, products, precision=lax.Precision.HIGHEST)
    right_side = jnp.einsum("ti,zbi->ztb", flux_sum, windows, precision=lax.Precision.HIGHEST)
    return (matrix, right_side)


def blocked_normals(weight_sum, flux_sum, rest_basis, shifts, first_wave, length):
    total_shifts = shifts.shape[0]
    block_size = 8
    grouped = shifts.reshape(total_shifts // block_size, block_size)

    def one_block(shift_block):
        return normal_terms(
            weight_sum, flux_sum, basis_windows(rest_basis, shift_block, first_wave, length)
        )

    matrix, right_side = lax.map(one_block, grouped)
    return (
        matrix.reshape((total_shifts,) + matrix.shape[2:]),
        right_side.reshape((total_shifts,) + right_side.shape[2:]),
    )


def fit_from(matrix, right_side):
    pairs = jnp.transpose(matrix, (2, 0, 1)).reshape(matrix.shape[2], -1)
    sides = jnp.transpose(right_side, (2, 0, 1)).reshape(right_side.shape[2], -1)
    gain = solve_normal(pairs, sides).reshape(matrix.shape[0], matrix.shape[1])
    return gain.T


def shards(
    exposure_flux,
    exposure_ivar,
    exposure_res,
    target_of_row,
    valid_of_row,
    rest_basis,
    redshift_shift,
):
    owners = lax.axis_size("tgt")
    device = lax.axis_index("tgt")
    row_count = exposure_flux.shape[0]
    wave_dev = exposure_flux.shape[1]
    capacity = 2 * row_count // owners
    own_target = lax.dynamic_slice_in_dim(target_of_row, device * row_count, row_count)
    owner_of = own_target // TGT_DEV
    row_ids = jnp.arange(row_count, dtype=jnp.int32)
    earlier = row_ids[None, :] < row_ids[:, None]
    position = jnp.sum(jnp.logical_and(owner_of[:, None] == owner_of[None, :], earlier), axis=1)
    slot_index = owner_of * capacity + position
    source_row = jnp.full((owners * capacity,), row_count, jnp.int32).at[slot_index].set(row_ids)

    def packed(values):
        gathered = jnp.take(values, source_row, axis=0, mode="fill", fill_value=0)
        return gathered.reshape((owners, capacity) + values.shape[1:])

    target_table = target_of_row.reshape(owners, row_count)
    is_mine = (target_table // TGT_DEV == device).astype(jnp.int32)
    before = jnp.cumsum(is_mine, axis=1) - is_mine
    matches = jnp.logical_and(
        is_mine[:, :, None] == 1,
        before[:, :, None] == jnp.arange(capacity, dtype=jnp.int32)[None, None, :],
    ).astype(jnp.int32)
    present = jnp.sum(matches, axis=1)
    local_target = jnp.sum(matches * (target_table % TGT_DEV)[:, :, None], axis=1)
    member = (
        jnp.logical_and(
            local_target[None] == jnp.arange(TGT_DEV, dtype=jnp.int32)[:, None, None],
            present[None] == 1,
        )
        .astype(jnp.float32)
        .reshape(TGT_DEV, owners * capacity)
    )
    outgoing = (packed(exposure_flux), packed(exposure_ivar), packed(exposure_res))
    got_flux, got_ivar, got_res = (
        lax.all_to_all(outgoing[0], "tgt", split_axis=0, concat_axis=0, tiled=True),
        lax.all_to_all(outgoing[1], "tgt", split_axis=0, concat_axis=0, tiled=True),
        lax.all_to_all(outgoing[2], "tgt", split_axis=0, concat_axis=0, tiled=True),
    )
    flag_table = valid_of_row.reshape(owners, row_count)
    usable = jnp.sum(matches * flag_table[:, :, None], axis=1)
    weight = got_ivar.astype(jnp.float32) * usable[:, :, None].astype(jnp.float32)
    flux_terms = weight * got_flux.astype(jnp.float32)
    res_terms = (weight[:, :, None, :] * got_res.astype(jnp.float32)).reshape(owners * capacity, -1)
    weight_sum = jnp.dot(
        member, weight.reshape(owners * capacity, wave_dev), precision=lax.Precision.HIGHEST
    )
    flux_sum = jnp.dot(
        member, flux_terms.reshape(owners * capacity, wave_dev), precision=lax.Precision.HIGHEST
    )
    res_sum = jnp.dot(member, res_terms, precision=lax.Precision.HIGHEST).reshape(
        TGT_DEV, NDIAG, wave_dev
    )
    coadd_flux = flux_sum / weight_sum
    coadd_res = (res_sum / weight_sum[:, None, :]).astype(jnp.bfloat16)
    band_index = lax.axis_index("band")
    weight_all, flux_all = (
        lax.all_gather(weight_sum.astype(jnp.bfloat16), "band", axis=1, tiled=True).astype(
            weight_sum.dtype
        ),
        lax.all_gather(flux_sum.astype(jnp.bfloat16), "band", axis=1, tiled=True).astype(
            flux_sum.dtype
        ),
    )
    shifts = lax.dynamic_slice_in_dim(redshift_shift, band_index * Z_DEV, Z_DEV)
    matrix, right_side = blocked_normals(
        weight_all, flux_all, rest_basis, shifts, 0, weight_all.shape[1]
    )
    fit_gain = fit_from(matrix, right_side)
    return (coadd_flux, coadd_res, fit_gain)

def as_bf16_parts(values, count):
    parts = []
    rest = values
    for step in range(count):
        part = rest.astype(jnp.bfloat16)
        parts.append(part)
        rest = rest - part.astype(jnp.float32)
    return parts


def exact_dot(left, right, dims, count):
    total = None
    for part in as_bf16_parts(left, count):
        term = lax.dot_general(part, right, (dims, ((), ())), preferred_element_type=jnp.float32)
        total = term if total is None else total + term
    return total


def fused_kernel(
    shift_s, target_v, valid_v, basis, ivar_any, flux_any, res_any,
    flux_out, res_out, gain_out,
    ivar, flux, res, weight, member, win,
    to_1, in_1, own_1, to_2, in_2, own_2, to_3, in_3, own_3,
    band_own, band_in, normal, right, inverse, res_done,
    l_sem, o_sem, send_sem, recv_sem, b_send, b_recv,
):
    owners, rows = target_v.shape
    channels, wave_dev = res.shape[0], res.shape[-1]
    pieces = channels + 2
    bands = lax.axis_size("band")
    waves = win.shape[2]
    basis_count = basis.shape[0]
    device = lax.axis_index("tgt")
    band = lax.axis_index("band")
    bits = [lax.rem(device // stride, 2) for stride in (1, 2, 4)]
    partners = [device + (1 - 2 * bit) * stride for bit, stride in zip(bits, (1, 2, 4))]

    def band_peer(d):
        return lax.rem(band + d, bands)

    loads = [
        pltpu.make_async_copy(ivar_any, ivar, l_sem.at[0]),
        pltpu.make_async_copy(flux_any, flux, l_sem.at[1]),
    ]
    for k in range(channels):
        loads.append(pltpu.make_async_copy(res_any.at[k], res.at[k], l_sem.at[k + 2]))
    for step in loads:
        step.start()

    stores = [
        pltpu.make_async_copy(res_done.at[k], res_out.at[k], o_sem.at[k]) for k in range(channels)
    ]
    barrier = pltpu.get_barrier_semaphore()
    near = [(partner, band) for partner in partners]
    near += [(device, band_peer(d)) for d in range(1, bands)]
    for place in near:
        pl.semaphore_signal(barrier, inc=1, device_id=place, device_id_type=MESH)

    def copy(source, target, send, recv, place):
        return pltpu.make_async_remote_copy(
            src_ref=source, dst_ref=target, send_sem=send, recv_sem=recv,
            device_id=place, device_id_type=MESH,
        )

    def order_of(p):
        return ORDERS[1] if p in Z_FIRST else ORDERS[0]

    rounds = ((to_1, in_1), (to_2, in_2), (to_3, in_3))
    copies = []
    for p in range(pieces):
        copies.append([
            copy(
                source.at[p], target.at[p], send_sem.at[p, r], recv_sem.at[p, r],
                (partners[order_of(p)[r]], band),
            )
            for r, (source, target) in enumerate(rounds)
        ])
    b_copies = [
        copy(band_own, band_in.at[d - 1], b_send.at[d - 1], b_recv.at[d - 1], (device, band_peer(d)))
        for d in range(1, bands)
    ]

    count = owners * TGT_DEV
    ids = lax.broadcasted_iota(jnp.int32, (count, rows), 0)
    own_target = target_v[pl.ds(device, 1), :]
    own_valid = valid_v[pl.ds(device, 1), :]

    def make_member(which):
        order = ORDERS[which]
        owner = jnp.zeros_like(ids)
        for r in range(3):
            mine = (ids // (count >> (r + 1))) % 2
            bit = mine * bits[order[r]] + (1 - mine) * (1 - bits[order[r]])
            owner = owner + bit * (1 << order[r])
        row_target = owner * TGT_DEV + ids % TGT_DEV
        table = jnp.where(row_target == own_target, own_valid, 0).astype(jnp.float32)
        table = table.astype(jnp.bfloat16)
        member[which] = jnp.concatenate([table, table], axis=1)
    dims = (((1,), (0,)), ((), ()))
    half, quarter, eighth = count // 2, count // 4, count // 8

    def prepare(p):
        loads[p].wait()
        which = 1 if p in Z_FIRST else 0
        if p == 0:
            weight[...] = ivar[...].astype(jnp.float32)
            part = lax.dot_general(
                member[which, :, 0:rows], ivar[...], dims, preferred_element_type=jnp.float32
            )
        else:
            values = flux[...] if p == 1 else res[p - 2]
            product = weight[...] * values.astype(jnp.float32)
            parts = jnp.concatenate(as_bf16_parts(product, 2), axis=0)
            part = lax.dot_general(member[which], parts, dims, preferred_element_type=jnp.float32)
        to_1[p] = part[0:half].astype(jnp.bfloat16)
        own_1[p] = part[half:]

    def round_1(p):
        copies[p][0].wait_recv()
        to_2[p] = (own_1[p, 0:quarter] + in_1[p, 0:quarter].astype(jnp.float32)).astype(jnp.bfloat16)
        copies[p][1].start()
        own_2[p] = own_1[p, quarter:] + in_1[p, quarter:].astype(jnp.float32)

    def round_2(p):
        copies[p][1].wait_recv()
        to_3[p] = (own_2[p, 0:eighth] + in_2[p, 0:eighth].astype(jnp.float32)).astype(jnp.bfloat16)
        copies[p][2].start()
        own_3[p] = own_2[p, eighth:] + in_2[p, eighth:].astype(jnp.float32)

    def round_3(p):
        copies[p][2].wait_recv()
        total = own_3[p] + in_3[p].astype(jnp.float32)
        if p < 2:
            band_own[p * TGT_DEV : (p + 1) * TGT_DEV, :] = total.astype(jnp.bfloat16)
            if p == 0:
                inverse[...] = 1.0 / total
            else:
                flux_out[...] = total * inverse[...]
        else:
            res_done[p - 2] = (total * inverse[...]).astype(jnp.bfloat16)
            stores[p - 2].start()

    def send_sums():
        for step in b_copies:
            step.start()

    def make_windows(first, last):
        ids8 = lax.broadcasted_iota(jnp.int32, (Z_DEV, 128), 0)
        shift = jnp.zeros((Z_DEV, 128), jnp.int32)
        for z in range(Z_DEV):
            shift = jnp.where(ids8 == z, shift_s[band * Z_DEV + z], shift)
        spare = basis.shape[1] - waves

        def one_basis(b, carry):
            rows_of = jnp.broadcast_to(basis[pl.ds(b, 1), :], (Z_DEV, basis.shape[1]))
            step = spare // 2
            while step >= 1:
                if step >= 128:
                    width = rows_of.shape[1] - step
                    moved, kept = rows_of[:, step:], rows_of[:, :width]
                else:
                    width = rows_of.shape[1]
                    moved, kept = pltpu.roll(rows_of, width - step, 1), rows_of
                wide = jnp.concatenate([shift] * (width // 128), axis=1)
                rows_of = jnp.where((wide & step) != 0, moved, kept)
                step //= 2
            win[b] = rows_of[:, :waves]
            return carry

        lax.fori_loop(first, last, one_basis, 0)

    def fit_block(d, part):
        if d == 0:
            source, place = band_own, band
        else:
            if part == 0:
                b_copies[d - 1].wait_recv()
            source, place = band_in.at[d - 1], lax.rem(band + (bands - d), bands)
        last = ((1,), (1,))
        steps = wave_dev // FIT_LANES // 2
        for step in range(part * steps, (part + 1) * steps):
            span = slice(step * FIT_LANES, (step + 1) * FIT_LANES)
            at = pl.multiple_of(place * wave_dev + step * FIT_LANES, FIT_LANES)
            bases = [win[b, :, pl.ds(at, FIT_LANES)] for b in range(basis_count)]
            pairs = [bases[int(b)] * bases[int(c)] for b, c in zip(pair_first, pair_second)]
            pairs.append(pairs[0])
            matrix = exact_dot(jnp.concatenate(pairs, axis=0), source[0:TGT_DEV, span], last, FIT_PARTS)
            sides = exact_dot(jnp.concatenate(bases, axis=0), source[TGT_DEV:, span], last, FIT_PARTS)
            if d == 0 and step == 0:
                normal[...] = matrix
                right[...] = sides
            else:
                normal[...] += matrix
                right[...] += sides

    def solve():
        matrix = [normal[Z_DEV * p : Z_DEV * (p + 1), :] for p in range(len(pair_first))]
        sides = [right[Z_DEV * b : Z_DEV * (b + 1), :] for b in range(basis_count)]
        gain_out[...] = solve_normal(matrix, jnp.stack(sides))

    make_member(0)
    prepare(0)
    pl.semaphore_wait(barrier, len(near))
    copies[0][0].start()
    make_member(1)
    for p in range(1, AHEAD):
        prepare(p)
        copies[p][0].start()
    middle = basis_count // 2
    jobs = [
        functools.partial(make_windows, 0, middle), functools.partial(make_windows, middle, basis_count)
    ]
    jobs += [send_sums] + [functools.partial(fit_block, d, h) for d in range(bands) for h in range(2)] + [solve]
    for p in range(pieces + 3):
        if p < pieces:
            round_1(p)
            if p + AHEAD < pieces:
                prepare(p + AHEAD)
                copies[p + AHEAD][0].start()
        if 1 <= p <= pieces:
            round_2(p - 1)
        if p >= 3:
            round_3(p - 3)
        for repeat in range((0, 1, 1, 0, 2, 2, 2)[p] if p < 7 else 1):
            if jobs:
                jobs.pop(0)()
    for step in b_copies + [step for piece in copies for step in piece]:
        step.wait_send()
    for step in stores:
        step.wait()


def finish_kernel(flux, res, gain, flux_out, res_out, gain_out, sem):
    steps = [
        pltpu.make_async_copy(res, res_out, sem.at[0]),
        pltpu.make_async_copy(flux, flux_out, sem.at[1]),
        pltpu.make_async_copy(gain, gain_out, sem.at[2]),
    ]
    for step in steps:
        step.start()
    for step in steps:
        step.wait()


def dense_shards(
    exposure_flux, exposure_ivar, exposure_res, target_of_row, valid_of_row, rest_basis, redshift_shift
):
    owners = lax.axis_size("tgt")
    bands = lax.axis_size("band")
    rows, wave_dev = exposure_flux.shape
    waves = wave_dev * bands
    basis_count = rest_basis.shape[0]
    pair_rows = Z_DEV * (len(pair_first) + 1)
    vmem = pl.BlockSpec(memory_space=pltpu.VMEM)
    smem = pl.BlockSpec(memory_space=pltpu.SMEM)
    hbm = pl.BlockSpec(memory_space=pl.ANY)
    half, full = jnp.bfloat16, jnp.float32
    block = (TGT_DEV, wave_dev)
    count = owners * TGT_DEV
    pieces = NDIAG + 2
    buffers = []
    for r in range(3):
        shape = (pieces, count >> (r + 1), wave_dev)
        buffers += [pltpu.VMEM(shape, half), pltpu.VMEM(shape, half), pltpu.VMEM(shape, full)]
    dma = pltpu.SemaphoreType.DMA
    coadd_flux, coadd_res, gain = pl.pallas_call(
        fused_kernel,
        out_shape=(
            jax.ShapeDtypeStruct(block, full),
            jax.ShapeDtypeStruct((NDIAG,) + block, half),
            jax.ShapeDtypeStruct((Z_DEV, TGT_DEV), full),
        ),
        in_specs=[smem, vmem, vmem, vmem, hbm, hbm, hbm],
        out_specs=(vmem, hbm, vmem),
        scratch_shapes=[
            pltpu.VMEM((rows, wave_dev), half),
            pltpu.VMEM((rows, wave_dev), half),
            pltpu.VMEM((NDIAG, rows, wave_dev), half),
            pltpu.VMEM((rows, wave_dev), full),
            pltpu.VMEM((2, count, 2 * rows), half),
            pltpu.VMEM((basis_count, Z_DEV, waves), full),
        ] + buffers + [
            pltpu.VMEM((2 * TGT_DEV, wave_dev), half),
            pltpu.VMEM((bands - 1, 2 * TGT_DEV, wave_dev), half),
            pltpu.VMEM((pair_rows, TGT_DEV), full),
            pltpu.VMEM((Z_DEV * basis_count, TGT_DEV), full),
            pltpu.VMEM(block, full),
            pltpu.VMEM((NDIAG,) + block, half),
            dma((pieces,)),
            dma((NDIAG,)),
            dma((pieces, 3)),
            dma((pieces, 3)),
            dma((bands - 1,)),
            dma((bands - 1,)),
        ],
        compiler_params=pltpu.CompilerParams(
            vmem_limit_bytes=VMEM_LIMIT, collective_id=0, has_side_effects=True
        ),
        name="coadd_and_fit",
    )(
        redshift_shift,
        target_of_row.reshape(owners, rows), valid_of_row.reshape(owners, rows), rest_basis,
        exposure_ivar, exposure_flux, jnp.transpose(exposure_res, (1, 0, 2)),
    )
    coadd_flux, coadd_res, gain = pl.pallas_call(
        finish_kernel,
        out_shape=(
            jax.ShapeDtypeStruct(block, full),
            jax.ShapeDtypeStruct(coadd_res.shape, half),
            jax.ShapeDtypeStruct(gain.shape, full),
        ),
        in_specs=[hbm] * 3,
        out_specs=(hbm, hbm, hbm),
        scratch_shapes=[dma((3,))],
        compiler_params=pltpu.CompilerParams(vmem_limit_bytes=VMEM_LIMIT),
        name="finish",
    )(coadd_flux, coadd_res, gain)
    return (coadd_flux, jnp.transpose(coadd_res, (1, 0, 2)), gain.T)


def solution(mesh):
    in_specs = (P("tgt", "band"), P("tgt", "band"), P("tgt", None, "band"), P(), P(), P(), P())
    out_specs = (P("tgt", "band"), P("tgt", None, "band"), P("tgt", "band"))
    owners = mesh.shape["tgt"]

    def whole(*args):
        rows = args[0].shape[0] // owners
        body = dense_shards if owners * TGT_DEV <= 2 * rows and owners == 8 else shards
        return jax.shard_map(
            body, mesh=mesh, in_specs=in_specs, out_specs=out_specs, check_vma=False
        )(*args)

    return whole
```

```python
import functools

import jax
import jax.numpy as jnp
import numpy as np
from jax import lax
from jax.experimental import pallas as pl
from jax.experimental.pallas import tpu as pltpu
from jax.sharding import PartitionSpec as P

TGT_DEV = 16
NDIAG = 11
Z_DEV = 8
FIT_LANES = 256
AHEAD = 3
FIT_PARTS = 2
ORDERS = ((0, 1, 2), (1, 0, 2))
Z_FIRST = ((2, 6, 10), (0, 4, 8))
VMEM_LIMIT = 60 * 1024 * 1024
MESH = pl.DeviceIdType.MESH


pair_first, pair_second = np.triu_indices(10)


def solve_normal(matrix, right_side):
    basis_count = right_side.shape[0]
    rows_of = [[None] * basis_count for column in range(basis_count)]
    for p in range(len(pair_first)):
        b = int(pair_first[p])
        c = int(pair_second[p])
        rows_of[b][c] = matrix[p]
        rows_of[c][b] = matrix[p]
    vector = [right_side[b] for b in range(basis_count)]
    for k in range(basis_count):
        inverse = 1.0 / rows_of[k][k]
        for r in range(k + 1, basis_count):
            factor = rows_of[r][k] * inverse
            for c in range(k + 1, basis_count):
                rows_of[r][c] = rows_of[r][c] - factor * rows_of[k][c]
            vector[r] = vector[r] - factor * vector[k]
    answer = [None] * basis_count
    for k in reversed(range(basis_count)):
        running = vector[k]
        for c in range(k + 1, basis_count):
            running = running - rows_of[k][c] * answer[c]
        answer[k] = running / rows_of[k][k]
    gain_total = right_side[0] * answer[0]
    for b in range(1, basis_count):
        gain_total = gain_total + right_side[b] * answer[b]
    return gain_total


def basis_windows(rest_basis, shifts, first_wave, length):

    def one_shift(shift_value):
        return lax.dynamic_slice_in_dim(rest_basis, first_wave + shift_value, length, axis=1)

    return jax.vmap(one_shift)(shifts)


def normal_terms(weight_sum, flux_sum, windows):
    products = windows[:, pair_first, :] * windows[:, pair_second, :]
    matrix = jnp.einsum("ti,zpi->ztp", weight_sum, products, precision=lax.Precision.HIGHEST)
    right_side = jnp.einsum("ti,zbi->ztb", flux_sum, windows, precision=lax.Precision.HIGHEST)
    return (matrix, right_side)


def blocked_normals(weight_sum, flux_sum, rest_basis, shifts, first_wave, length):
    total_shifts = shifts.shape[0]
    block_size = 8
    grouped = shifts.reshape(total_shifts // block_size, block_size)

    def one_block(shift_block):
        return normal_terms(
            weight_sum, flux_sum, basis_windows(rest_basis, shift_block, first_wave, length)
        )

    matrix, right_side = lax.map(one_block, grouped)
    return (
        matrix.reshape((total_shifts,) + matrix.shape[2:]),
        right_side.reshape((total_shifts,) + right_side.shape[2:]),
    )


def fit_from(matrix, right_side):
    pairs = jnp.transpose(matrix, (2, 0, 1)).reshape(matrix.shape[2], -1)
    sides = jnp.transpose(right_side, (2, 0, 1)).reshape(right_side.shape[2], -1)
    gain = solve_normal(pairs, sides).reshape(matrix.shape[0], matrix.shape[1])
    return gain.T


def shards(
    exposure_flux,
    exposure_ivar,
    exposure_res,
    target_of_row,
    valid_of_row,
    rest_basis,
    redshift_shift,
):
    owners = lax.axis_size("tgt")
    device = lax.axis_index("tgt")
    row_count = exposure_flux.shape[0]
    wave_dev = exposure_flux.shape[1]
    capacity = 2 * row_count // owners
    own_target = lax.dynamic_slice_in_dim(target_of_row, device * row_count, row_count)
    owner_of = own_target // TGT_DEV
    row_ids = jnp.arange(row_count, dtype=jnp.int32)
    earlier = row_ids[None, :] < row_ids[:, None]
    position = jnp.sum(jnp.logical_and(owner_of[:, None] == owner_of[None, :], earlier), axis=1)
    slot_index = owner_of * capacity + position
    source_row = jnp.full((owners * capacity,), row_count, jnp.int32).at[slot_index].set(row_ids)

    def packed(values):
        gathered = jnp.take(values, source_row, axis=0, mode="fill", fill_value=0)
        return gathered.reshape((owners, capacity) + values.shape[1:])

    target_table = target_of_row.reshape(owners, row_count)
    is_mine = (target_table // TGT_DEV == device).astype(jnp.int32)
    before = jnp.cumsum(is_mine, axis=1) - is_mine
    matches = jnp.logical_and(
        is_mine[:, :, None] == 1,
        before[:, :, None] == jnp.arange(capacity, dtype=jnp.int32)[None, None, :],
    ).astype(jnp.int32)
    present = jnp.sum(matches, axis=1)
    local_target = jnp.sum(matches * (target_table % TGT_DEV)[:, :, None], axis=1)
    member = (
        jnp.logical_and(
            local_target[None] == jnp.arange(TGT_DEV, dtype=jnp.int32)[:, None, None],
            present[None] == 1,
        )
        .astype(jnp.float32)
        .reshape(TGT_DEV, owners * capacity)
    )
    outgoing = (packed(exposure_flux), packed(exposure_ivar), packed(exposure_res))
    got_flux, got_ivar, got_res = (
        lax.all_to_all(outgoing[0], "tgt", split_axis=0, concat_axis=0, tiled=True),
        lax.all_to_all(outgoing[1], "tgt", split_axis=0, concat_axis=0, tiled=True),
        lax.all_to_all(outgoing[2], "tgt", split_axis=0, concat_axis=0, tiled=True),
    )
    flag_table = valid_of_row.reshape(owners, row_count)
    usable = jnp.sum(matches * flag_table[:, :, None], axis=1)
    weight = got_ivar.astype(jnp.float32) * usable[:, :, None].astype(jnp.float32)
    flux_terms = weight * got_flux.astype(jnp.float32)
    res_terms = (weight[:, :, None, :] * got_res.astype(jnp.float32)).reshape(owners * capacity, -1)
    weight_sum = jnp.dot(
        member, weight.reshape(owners * capacity, wave_dev), precision=lax.Precision.HIGHEST
    )
    flux_sum = jnp.dot(
        member, flux_terms.reshape(owners * capacity, wave_dev), precision=lax.Precision.HIGHEST
    )
    res_sum = jnp.dot(member, res_terms, precision=lax.Precision.HIGHEST).reshape(
        TGT_DEV, NDIAG, wave_dev
    )
    coadd_flux = flux_sum / weight_sum
    coadd_res = (res_sum / weight_sum[:, None, :]).astype(jnp.bfloat16)
    band_index = lax.axis_index("band")
    weight_all, flux_all = (
        lax.all_gather(weight_sum.astype(jnp.bfloat16), "band", axis=1, tiled=True).astype(
            weight_sum.dtype
        ),
        lax.all_gather(flux_sum.astype(jnp.bfloat16), "band", axis=1, tiled=True).astype(
            flux_sum.dtype
        ),
    )
    shifts = lax.dynamic_slice_in_dim(redshift_shift, band_index * Z_DEV, Z_DEV)
    matrix, right_side = blocked_normals(
        weight_all, flux_all, rest_basis, shifts, 0, weight_all.shape[1]
    )
    fit_gain = fit_from(matrix, right_side)
    return (coadd_flux, coadd_res, fit_gain)

def as_bf16_parts(values, count):
    parts = []
    rest = values
    for step in range(count):
        part = rest.astype(jnp.bfloat16)
        parts.append(part)
        rest = rest - part.astype(jnp.float32)
    return parts


def exact_dot(left, right, dims, count):
    total = None
    for part in as_bf16_parts(left, count):
        term = lax.dot_general(part, right, (dims, ((), ())), preferred_element_type=jnp.float32)
        total = term if total is None else total + term
    return total


def fused_kernel(
    shift_s, target_v, valid_v, basis, ivar_any, flux_any, res_any,
    flux_out, res_out, gain_out,
    ivar, flux, res, weight, member, win,
    to_1, in_1, own_1, to_2, in_2, own_2, to_3, in_3, own_3,
    band_own, band_in, normal, right, inverse,
    l_sem, send_sem, recv_sem, b_send, b_recv,
):
    owners, rows = target_v.shape
    channels, wave_dev = res.shape[0], res.shape[-1]
    pieces = channels + 2
    bands = lax.axis_size("band")
    waves = win.shape[2]
    basis_count = basis.shape[0]
    device = lax.axis_index("tgt")
    band = lax.axis_index("band")
    bits = [lax.rem(device // stride, 2) for stride in (1, 2, 4)]
    partners = [device + (1 - 2 * bit) * stride for bit, stride in zip(bits, (1, 2, 4))]

    def band_peer(d):
        return lax.rem(band + d, bands)

    loads = [
        pltpu.make_async_copy(ivar_any, ivar, l_sem.at[0]),
        pltpu.make_async_copy(flux_any, flux, l_sem.at[1]),
    ]
    for k in range(channels):
        loads.append(pltpu.make_async_copy(res_any.at[k], res.at[k], l_sem.at[k + 2]))
    for step in loads:
        step.start()

    barrier = pltpu.get_barrier_semaphore()
    near = [(partner, band) for partner in partners]
    near += [(device, band_peer(d)) for d in range(1, bands)]
    for place in near:
        pl.semaphore_signal(barrier, inc=1, device_id=place, device_id_type=MESH)

    def copy(source, target, send, recv, place):
        return pltpu.make_async_remote_copy(
            src_ref=source, dst_ref=target, send_sem=send, recv_sem=recv,
            device_id=place, device_id_type=MESH,
        )

    core = lax.rem(band, 2)

    def order_of(p):
        if p in Z_FIRST[0]:
            return 1 - core
        return core if p in Z_FIRST[1] else 0

    def partner_of(p, r):
        which = order_of(p)
        first, second = partners[ORDERS[0][r]], partners[ORDERS[1][r]]
        return (1 - which) * first + which * second

    rounds = ((to_1, in_1), (to_2, in_2), (to_3, in_3))
    copies = []
    for p in range(pieces):
        copies.append([
            copy(
                source.at[p], target.at[p], send_sem.at[p, r], recv_sem.at[p, r],
                (partner_of(p, r), band),
            )
            for r, (source, target) in enumerate(rounds)
        ])
    b_copies = [
        copy(band_own, band_in.at[d - 1], b_send.at[d - 1], b_recv.at[d - 1], (device, band_peer(d)))
        for d in range(1, bands)
    ]

    count = owners * TGT_DEV
    ids = lax.broadcasted_iota(jnp.int32, (count, rows), 0)
    own_target = target_v[pl.ds(device, 1), :]
    own_valid = valid_v[pl.ds(device, 1), :]

    def make_member(which):
        order = ORDERS[which]
        owner = jnp.zeros_like(ids)
        for r in range(3):
            mine = (ids // (count >> (r + 1))) % 2
            bit = mine * bits[order[r]] + (1 - mine) * (1 - bits[order[r]])
            owner = owner + bit * (1 << order[r])
        row_target = owner * TGT_DEV + ids % TGT_DEV
        table = jnp.where(row_target == own_target, own_valid, 0).astype(jnp.float32)
        table = table.astype(jnp.bfloat16)
        member[which] = jnp.concatenate([table, table], axis=1)
    dims = (((1,), (0,)), ((), ()))
    half, quarter, eighth = count // 2, count // 4, count // 8

    def prepare(p):
        loads[p].wait()
        which = order_of(p)
        if p == 0:
            weight[...] = ivar[...].astype(jnp.float32)
            part = lax.dot_general(
                member[which, :, 0:rows], ivar[...], dims, preferred_element_type=jnp.float32
            )
        else:
            values = flux[...] if p == 1 else res[p - 2]
            product = weight[...] * values.astype(jnp.float32)
            parts = jnp.concatenate(as_bf16_parts(product, 2), axis=0)
            part = lax.dot_general(member[which], parts, dims, preferred_element_type=jnp.float32)
        to_1[p] = part[0:half].astype(jnp.bfloat16)
        own_1[p] = part[half:]

    def round_1(p):
        copies[p][0].wait_recv()
        if p + AHEAD < pieces:
            copies[p + AHEAD][0].start()
        to_2[p] = (own_1[p, 0:quarter] + in_1[p, 0:quarter].astype(jnp.float32)).astype(jnp.bfloat16)
        copies[p][1].start()
        own_2[p] = own_1[p, quarter:] + in_1[p, quarter:].astype(jnp.float32)

    def round_2(p):
        copies[p][1].wait_recv()
        to_3[p] = (own_2[p, 0:eighth] + in_2[p, 0:eighth].astype(jnp.float32)).astype(jnp.bfloat16)
        copies[p][2].start()
        own_3[p] = own_2[p, eighth:] + in_2[p, eighth:].astype(jnp.float32)

    def round_3(p):
        copies[p][2].wait_recv()
        total = own_3[p] + in_3[p].astype(jnp.float32)
        if p < 2:
            band_own[p * TGT_DEV : (p + 1) * TGT_DEV, :] = total.astype(jnp.bfloat16)
            if p == 0:
                inverse[...] = 1.0 / total
            else:
                flux_out[...] = total * inverse[...]
        else:
            res_out[p - 2] = (total * inverse[...]).astype(jnp.bfloat16)

    def send_sums():
        for step in b_copies:
            step.start()

    def make_windows(first, last):
        ids8 = lax.broadcasted_iota(jnp.int32, (Z_DEV, 128), 0)
        shift = jnp.zeros((Z_DEV, 128), jnp.int32)
        for z in range(Z_DEV):
            shift = jnp.where(ids8 == z, shift_s[band * Z_DEV + z], shift)
        spare = basis.shape[1] - waves

        def one_basis(b, carry):
            rows_of = jnp.broadcast_to(basis[pl.ds(b, 1), :], (Z_DEV, basis.shape[1]))
            step = spare // 2
            while step >= 1:
                if step >= 128:
                    width = rows_of.shape[1] - step
                    moved, kept = rows_of[:, step:], rows_of[:, :width]
                else:
                    width = rows_of.shape[1]
                    moved, kept = pltpu.roll(rows_of, width - step, 1), rows_of
                wide = jnp.concatenate([shift] * (width // 128), axis=1)
                rows_of = jnp.where((wide & step) != 0, moved, kept)
                step //= 2
            win[b] = rows_of[:, :waves]
            return carry

        lax.fori_loop(first, last, one_basis, 0)

    def fit_block(d, part):
        if d == 0:
            source, place = band_own, band
        else:
            if part == 0:
                b_copies[d - 1].wait_recv()
            source, place = band_in.at[d - 1], lax.rem(band + (bands - d), bands)
        last = ((1,), (1,))
        steps = wave_dev // FIT_LANES // 2
        for step in range(part * steps, (part + 1) * steps):
            span = slice(step * FIT_LANES, (step + 1) * FIT_LANES)
            at = pl.multiple_of(place * wave_dev + step * FIT_LANES, FIT_LANES)
            bases = [win[b, :, pl.ds(at, FIT_LANES)] for b in range(basis_count)]
            pairs = [bases[int(b)] * bases[int(c)] for b, c in zip(pair_first, pair_second)]
            pairs.append(pairs[0])
            matrix = exact_dot(jnp.concatenate(pairs, axis=0), source[0:TGT_DEV, span], last, FIT_PARTS)
            sides = exact_dot(jnp.concatenate(bases, axis=0), source[TGT_DEV:, span], last, FIT_PARTS)
            if d == 0 and step == 0:
                normal[...] = matrix
                right[...] = sides
            else:
                normal[...] += matrix
                right[...] += sides

    def solve():
        matrix = [normal[Z_DEV * p : Z_DEV * (p + 1), :] for p in range(len(pair_first))]
        sides = [right[Z_DEV * b : Z_DEV * (b + 1), :] for b in range(basis_count)]
        gain_out[...] = solve_normal(matrix, jnp.stack(sides))

    make_member(0)
    make_member(1)
    prepare(0)
    pl.semaphore_wait(barrier, len(near))
    copies[0][0].start()
    for p in range(1, AHEAD):
        prepare(p)
        copies[p][0].start()
    prepare(AHEAD)
    middle = basis_count // 2
    jobs = [
        functools.partial(make_windows, 0, middle), functools.partial(make_windows, middle, basis_count)
    ]
    jobs += [send_sums] + [functools.partial(fit_block, d, h) for d in range(bands) for h in range(2)] + [solve]
    for p in range(pieces + 3):
        if p < pieces:
            round_1(p)
            if p + AHEAD + 1 < pieces:
                prepare(p + AHEAD + 1)
        if 1 <= p <= pieces:
            round_2(p - 1)
        if p >= 3:
            round_3(p - 3)
        for repeat in range((0, 1, 1, 0, 2, 2, 2)[p] if p < 7 else 1):
            if jobs:
                jobs.pop(0)()
    for step in b_copies + [step for piece in copies for step in piece]:
        step.wait_send()


def finish_kernel(flux, res, gain, flux_out, res_out, gain_out):
    flux_out[...] = flux[...]
    res_out[...] = res[...]
    gain_out[...] = gain[...]


def dense_shards(
    exposure_flux, exposure_ivar, exposure_res, target_of_row, valid_of_row, rest_basis, redshift_shift
):
    owners = lax.axis_size("tgt")
    bands = lax.axis_size("band")
    rows, wave_dev = exposure_flux.shape
    waves = wave_dev * bands
    basis_count = rest_basis.shape[0]
    pair_rows = Z_DEV * (len(pair_first) + 1)
    vmem = pl.BlockSpec(memory_space=pltpu.VMEM)
    smem = pl.BlockSpec(memory_space=pltpu.SMEM)
    hbm = pl.BlockSpec(memory_space=pl.ANY)
    half, full = jnp.bfloat16, jnp.float32
    block = (TGT_DEV, wave_dev)
    count = owners * TGT_DEV
    pieces = NDIAG + 2
    buffers = []
    for r in range(3):
        shape = (pieces, count >> (r + 1), wave_dev)
        buffers += [pltpu.VMEM(shape, half), pltpu.VMEM(shape, half), pltpu.VMEM(shape, full)]
    dma = pltpu.SemaphoreType.DMA
    coadd_flux, coadd_res, gain = pl.pallas_call(
        fused_kernel,
        out_shape=(
            jax.ShapeDtypeStruct(block, full),
            jax.ShapeDtypeStruct((NDIAG,) + block, half),
            jax.ShapeDtypeStruct((Z_DEV, TGT_DEV), full),
        ),
        in_specs=[smem, vmem, vmem, vmem, hbm, hbm, hbm],
        out_specs=(vmem, vmem, vmem),
        scratch_shapes=[
            pltpu.VMEM((rows, wave_dev), half),
            pltpu.VMEM((rows, wave_dev), half),
            pltpu.VMEM((NDIAG, rows, wave_dev), half),
            pltpu.VMEM((rows, wave_dev), full),
            pltpu.VMEM((2, count, 2 * rows), half),
            pltpu.VMEM((basis_count, Z_DEV, waves), full),
        ] + buffers + [
            pltpu.VMEM((2 * TGT_DEV, wave_dev), half),
            pltpu.VMEM((bands - 1, 2 * TGT_DEV, wave_dev), half),
            pltpu.VMEM((pair_rows, TGT_DEV), full),
            pltpu.VMEM((Z_DEV * basis_count, TGT_DEV), full),
            pltpu.VMEM(block, full),
            dma((pieces,)),
            dma((pieces, 3)),
            dma((pieces, 3)),
            dma((bands - 1,)),
            dma((bands - 1,)),
        ],
        compiler_params=pltpu.CompilerParams(
            vmem_limit_bytes=VMEM_LIMIT, collective_id=0, has_side_effects=True
        ),
        name="coadd_and_fit",
    )(
        redshift_shift,
        target_of_row.reshape(owners, rows), valid_of_row.reshape(owners, rows), rest_basis,
        exposure_ivar, exposure_flux, jnp.transpose(exposure_res, (1, 0, 2)),
    )
    coadd_flux, coadd_res, gain = pl.pallas_call(
        finish_kernel,
        out_shape=(
            jax.ShapeDtypeStruct(block, full),
            jax.ShapeDtypeStruct(coadd_res.shape, half),
            jax.ShapeDtypeStruct(gain.shape, full),
        ),
        in_specs=[vmem] * 3,
        out_specs=(vmem, vmem, vmem),
        compiler_params=pltpu.CompilerParams(vmem_limit_bytes=VMEM_LIMIT),
        name="finish",
    )(coadd_flux, coadd_res, gain)
    return (coadd_flux, jnp.transpose(coadd_res, (1, 0, 2)), gain.T)


def solution(mesh):
    in_specs = (P("tgt", "band"), P("tgt", "band"), P("tgt", None, "band"), P(), P(), P(), P())
    out_specs = (P("tgt", "band"), P("tgt", None, "band"), P("tgt", "band"))
    owners = mesh.shape["tgt"]

    def whole(*args):
        rows = args[0].shape[0] // owners
        body = dense_shards if owners * TGT_DEV <= 2 * rows and owners == 8 else shards
        return jax.shard_map(
            body, mesh=mesh, in_specs=in_specs, out_specs=out_specs, check_vma=False
        )(*args)

    return whole
```

```python
import functools

import jax
import jax.numpy as jnp
import numpy as np
from jax import lax
from jax.experimental import pallas as pl
from jax.experimental.pallas import tpu as pltpu
from jax.sharding import PartitionSpec as P

TGT_DEV = 16
NDIAG = 11
Z_DEV = 8
FIT_LANES = 256
AHEAD = 2
FIT_PARTS = 2
ORDERS = ((0, 1, 2), (1, 0, 2))
Z_FIRST = ((2, 6, 10), (0, 4, 8))
VMEM_LIMIT = 60 * 1024 * 1024
MESH = pl.DeviceIdType.MESH


pair_first, pair_second = np.triu_indices(10)


def solve_normal(matrix, right_side):
    basis_count = right_side.shape[0]
    rows_of = [[None] * basis_count for column in range(basis_count)]
    for p in range(len(pair_first)):
        b = int(pair_first[p])
        c = int(pair_second[p])
        rows_of[b][c] = matrix[p]
        rows_of[c][b] = matrix[p]
    vector = [right_side[b] for b in range(basis_count)]
    for k in range(basis_count):
        inverse = 1.0 / rows_of[k][k]
        for r in range(k + 1, basis_count):
            factor = rows_of[r][k] * inverse
            for c in range(k + 1, basis_count):
                rows_of[r][c] = rows_of[r][c] - factor * rows_of[k][c]
            vector[r] = vector[r] - factor * vector[k]
    answer = [None] * basis_count
    for k in reversed(range(basis_count)):
        running = vector[k]
        for c in range(k + 1, basis_count):
            running = running - rows_of[k][c] * answer[c]
        answer[k] = running / rows_of[k][k]
    gain_total = right_side[0] * answer[0]
    for b in range(1, basis_count):
        gain_total = gain_total + right_side[b] * answer[b]
    return gain_total


def basis_windows(rest_basis, shifts, first_wave, length):

    def one_shift(shift_value):
        return lax.dynamic_slice_in_dim(rest_basis, first_wave + shift_value, length, axis=1)

    return jax.vmap(one_shift)(shifts)


def normal_terms(weight_sum, flux_sum, windows):
    products = windows[:, pair_first, :] * windows[:, pair_second, :]
    matrix = jnp.einsum("ti,zpi->ztp", weight_sum, products, precision=lax.Precision.HIGHEST)
    right_side = jnp.einsum("ti,zbi->ztb", flux_sum, windows, precision=lax.Precision.HIGHEST)
    return (matrix, right_side)


def blocked_normals(weight_sum, flux_sum, rest_basis, shifts, first_wave, length):
    total_shifts = shifts.shape[0]
    block_size = 8
    grouped = shifts.reshape(total_shifts // block_size, block_size)

    def one_block(shift_block):
        return normal_terms(
            weight_sum, flux_sum, basis_windows(rest_basis, shift_block, first_wave, length)
        )

    matrix, right_side = lax.map(one_block, grouped)
    return (
        matrix.reshape((total_shifts,) + matrix.shape[2:]),
        right_side.reshape((total_shifts,) + right_side.shape[2:]),
    )


def fit_from(matrix, right_side):
    pairs = jnp.transpose(matrix, (2, 0, 1)).reshape(matrix.shape[2], -1)
    sides = jnp.transpose(right_side, (2, 0, 1)).reshape(right_side.shape[2], -1)
    gain = solve_normal(pairs, sides).reshape(matrix.shape[0], matrix.shape[1])
    return gain.T


def shards(
    exposure_flux,
    exposure_ivar,
    exposure_res,
    target_of_row,
    valid_of_row,
    rest_basis,
    redshift_shift,
):
    owners = lax.axis_size("tgt")
    device = lax.axis_index("tgt")
    row_count = exposure_flux.shape[0]
    wave_dev = exposure_flux.shape[1]
    capacity = 2 * row_count // owners
    own_target = lax.dynamic_slice_in_dim(target_of_row, device * row_count, row_count)
    owner_of = own_target // TGT_DEV
    row_ids = jnp.arange(row_count, dtype=jnp.int32)
    earlier = row_ids[None, :] < row_ids[:, None]
    position = jnp.sum(jnp.logical_and(owner_of[:, None] == owner_of[None, :], earlier), axis=1)
    slot_index = owner_of * capacity + position
    source_row = jnp.full((owners * capacity,), row_count, jnp.int32).at[slot_index].set(row_ids)

    def packed(values):
        gathered = jnp.take(values, source_row, axis=0, mode="fill", fill_value=0)
        return gathered.reshape((owners, capacity) + values.shape[1:])

    target_table = target_of_row.reshape(owners, row_count)
    is_mine = (target_table // TGT_DEV == device).astype(jnp.int32)
    before = jnp.cumsum(is_mine, axis=1) - is_mine
    matches = jnp.logical_and(
        is_mine[:, :, None] == 1,
        before[:, :, None] == jnp.arange(capacity, dtype=jnp.int32)[None, None, :],
    ).astype(jnp.int32)
    present = jnp.sum(matches, axis=1)
    local_target = jnp.sum(matches * (target_table % TGT_DEV)[:, :, None], axis=1)
    member = (
        jnp.logical_and(
            local_target[None] == jnp.arange(TGT_DEV, dtype=jnp.int32)[:, None, None],
            present[None] == 1,
        )
        .astype(jnp.float32)
        .reshape(TGT_DEV, owners * capacity)
    )
    outgoing = (packed(exposure_flux), packed(exposure_ivar), packed(exposure_res))
    got_flux, got_ivar, got_res = (
        lax.all_to_all(outgoing[0], "tgt", split_axis=0, concat_axis=0, tiled=True),
        lax.all_to_all(outgoing[1], "tgt", split_axis=0, concat_axis=0, tiled=True),
        lax.all_to_all(outgoing[2], "tgt", split_axis=0, concat_axis=0, tiled=True),
    )
    flag_table = valid_of_row.reshape(owners, row_count)
    usable = jnp.sum(matches * flag_table[:, :, None], axis=1)
    weight = got_ivar.astype(jnp.float32) * usable[:, :, None].astype(jnp.float32)
    flux_terms = weight * got_flux.astype(jnp.float32)
    res_terms = (weight[:, :, None, :] * got_res.astype(jnp.float32)).reshape(owners * capacity, -1)
    weight_sum = jnp.dot(
        member, weight.reshape(owners * capacity, wave_dev), precision=lax.Precision.HIGHEST
    )
    flux_sum = jnp.dot(
        member, flux_terms.reshape(owners * capacity, wave_dev), precision=lax.Precision.HIGHEST
    )
    res_sum = jnp.dot(member, res_terms, precision=lax.Precision.HIGHEST).reshape(
        TGT_DEV, NDIAG, wave_dev
    )
    coadd_flux = flux_sum / weight_sum
    coadd_res = (res_sum / weight_sum[:, None, :]).astype(jnp.bfloat16)
    band_index = lax.axis_index("band")
    weight_all, flux_all = (
        lax.all_gather(weight_sum.astype(jnp.bfloat16), "band", axis=1, tiled=True).astype(
            weight_sum.dtype
        ),
        lax.all_gather(flux_sum.astype(jnp.bfloat16), "band", axis=1, tiled=True).astype(
            flux_sum.dtype
        ),
    )
    shifts = lax.dynamic_slice_in_dim(redshift_shift, band_index * Z_DEV, Z_DEV)
    matrix, right_side = blocked_normals(
        weight_all, flux_all, rest_basis, shifts, 0, weight_all.shape[1]
    )
    fit_gain = fit_from(matrix, right_side)
    return (coadd_flux, coadd_res, fit_gain)

def as_bf16_parts(values, count):
    parts = []
    rest = values
    for step in range(count):
        part = rest.astype(jnp.bfloat16)
        parts.append(part)
        rest = rest - part.astype(jnp.float32)
    return parts


def exact_dot(left, right, dims, count):
    total = None
    for part in as_bf16_parts(left, count):
        term = lax.dot_general(part, right, (dims, ((), ())), preferred_element_type=jnp.float32)
        total = term if total is None else total + term
    return total


def fused_kernel(
    shift_s, target_v, valid_v, basis, ivar_any, flux_any, res_any,
    flux_out, res_out, gain_out,
    ivar, flux, res, weight, member, win,
    to_1, in_1, own_1, to_2, in_2, own_2, to_3, in_3, own_3,
    band_own, band_in, normal, right, inverse,
    l_sem, send_sem, recv_sem, b_send, b_recv,
):
    owners, rows = target_v.shape
    channels, wave_dev = res.shape[0], res.shape[-1]
    pieces = channels + 2
    bands = lax.axis_size("band")
    waves = win.shape[2]
    basis_count = basis.shape[0]
    device = lax.axis_index("tgt")
    band = lax.axis_index("band")
    bits = [lax.rem(device // stride, 2) for stride in (1, 2, 4)]
    partners = [device + (1 - 2 * bit) * stride for bit, stride in zip(bits, (1, 2, 4))]

    def band_peer(d):
        return lax.rem(band + d, bands)

    loads = [
        pltpu.make_async_copy(ivar_any, ivar, l_sem.at[0]),
        pltpu.make_async_copy(flux_any, flux, l_sem.at[1]),
    ]
    for k in range(channels):
        loads.append(pltpu.make_async_copy(res_any.at[k], res.at[k], l_sem.at[k + 2]))
    for step in loads:
        step.start()

    barrier = pltpu.get_barrier_semaphore()
    near = [(partner, band) for partner in partners]
    near += [(device, band_peer(d)) for d in range(1, bands)]
    for place in near:
        pl.semaphore_signal(barrier, inc=1, device_id=place, device_id_type=MESH)

    def copy(source, target, send, recv, place):
        return pltpu.make_async_remote_copy(
            src_ref=source, dst_ref=target, send_sem=send, recv_sem=recv,
            device_id=place, device_id_type=MESH,
        )

    core = lax.rem(band, 2)

    def order_of(p):
        if p in Z_FIRST[0]:
            return 1 - core
        return core if p in Z_FIRST[1] else 0

    def partner_of(p, r):
        which = order_of(p)
        first, second = partners[ORDERS[0][r]], partners[ORDERS[1][r]]
        return (1 - which) * first + which * second

    rounds = ((to_1, in_1), (to_2, in_2), (to_3, in_3))
    copies = []
    for p in range(pieces):
        copies.append([
            copy(
                source.at[p], target.at[p], send_sem.at[p, r], recv_sem.at[p, r],
                (partner_of(p, r), band),
            )
            for r, (source, target) in enumerate(rounds)
        ])
    b_copies = [
        copy(band_own, band_in.at[d - 1], b_send.at[d - 1], b_recv.at[d - 1], (device, band_peer(d)))
        for d in range(1, bands)
    ]

    count = owners * TGT_DEV
    ids = lax.broadcasted_iota(jnp.int32, (count, rows), 0)
    own_target = target_v[pl.ds(device, 1), :]
    own_valid = valid_v[pl.ds(device, 1), :]

    def make_member(which):
        order = ORDERS[which]
        owner = jnp.zeros_like(ids)
        for r in range(3):
            mine = (ids // (count >> (r + 1))) % 2
            bit = mine * bits[order[r]] + (1 - mine) * (1 - bits[order[r]])
            owner = owner + bit * (1 << order[r])
        row_target = owner * TGT_DEV + ids % TGT_DEV
        table = jnp.where(row_target == own_target, own_valid, 0).astype(jnp.float32)
        table = table.astype(jnp.bfloat16)
        member[which] = jnp.concatenate([table, table], axis=1)
    dims = (((1,), (0,)), ((), ()))
    half, quarter, eighth = count // 2, count // 4, count // 8

    def prepare(p):
        loads[p].wait()
        which = order_of(p)
        if p == 0:
            weight[...] = ivar[...].astype(jnp.float32)
            part = lax.dot_general(
                member[which, :, 0:rows], ivar[...], dims, preferred_element_type=jnp.float32
            )
        else:
            values = flux[...] if p == 1 else res[p - 2]
            product = weight[...] * values.astype(jnp.float32)
            parts = jnp.concatenate(as_bf16_parts(product, 2), axis=0)
            part = lax.dot_general(member[which], parts, dims, preferred_element_type=jnp.float32)
        to_1[p] = part[0:half].astype(jnp.bfloat16)
        own_1[p] = part[half:]

    def round_1(p):
        copies[p][0].wait_recv()
        if p + AHEAD < pieces:
            copies[p + AHEAD][0].start()
        to_2[p] = (own_1[p, 0:quarter] + in_1[p, 0:quarter].astype(jnp.float32)).astype(jnp.bfloat16)
        copies[p][1].start()
        own_2[p] = own_1[p, quarter:] + in_1[p, quarter:].astype(jnp.float32)

    def round_2(p):
        copies[p][1].wait_recv()
        to_3[p] = (own_2[p, 0:eighth] + in_2[p, 0:eighth].astype(jnp.float32)).astype(jnp.bfloat16)
        copies[p][2].start()
        own_3[p] = own_2[p, eighth:] + in_2[p, eighth:].astype(jnp.float32)

    def round_3(p):
        copies[p][2].wait_recv()
        total = own_3[p] + in_3[p].astype(jnp.float32)
        if p < 2:
            band_own[p * TGT_DEV : (p + 1) * TGT_DEV, :] = total.astype(jnp.bfloat16)
            if p == 0:
                inverse[...] = 1.0 / total
            else:
                flux_out[...] = total * inverse[...]
        else:
            res_out[p - 2] = (total * inverse[...]).astype(jnp.bfloat16)

    def send_sums():
        for step in b_copies:
            step.start()

    def make_windows(first, last):
        ids8 = lax.broadcasted_iota(jnp.int32, (Z_DEV, 128), 0)
        shift = jnp.zeros((Z_DEV, 128), jnp.int32)
        for z in range(Z_DEV):
            shift = jnp.where(ids8 == z, shift_s[band * Z_DEV + z], shift)
        spare = basis.shape[1] - waves

        def one_basis(b, carry):
            rows_of = jnp.broadcast_to(basis[pl.ds(b, 1), :], (Z_DEV, basis.shape[1]))
            step = spare // 2
            while step >= 1:
                if step >= 128:
                    width = rows_of.shape[1] - step
                    moved, kept = rows_of[:, step:], rows_of[:, :width]
                else:
                    width = rows_of.shape[1]
                    moved, kept = pltpu.roll(rows_of, width - step, 1), rows_of
                wide = jnp.concatenate([shift] * (width // 128), axis=1)
                rows_of = jnp.where((wide & step) != 0, moved, kept)
                step //= 2
            win[b] = rows_of[:, :waves]
            return carry

        lax.fori_loop(first, last, one_basis, 0)

    def fit_block(d, part):
        if d == 0:
            source, place = band_own, band
        else:
            if part == 0:
                b_copies[d - 1].wait_recv()
            source, place = band_in.at[d - 1], lax.rem(band + (bands - d), bands)
        last = ((1,), (1,))
        steps = wave_dev // FIT_LANES // 2
        for step in range(part * steps, (part + 1) * steps):
            span = slice(step * FIT_LANES, (step + 1) * FIT_LANES)
            at = pl.multiple_of(place * wave_dev + step * FIT_LANES, FIT_LANES)
            bases = [win[b, :, pl.ds(at, FIT_LANES)] for b in range(basis_count)]
            pairs = [bases[int(b)] * bases[int(c)] for b, c in zip(pair_first, pair_second)]
            pairs.append(pairs[0])
            matrix = exact_dot(jnp.concatenate(pairs, axis=0), source[0:TGT_DEV, span], last, FIT_PARTS)
            sides = exact_dot(jnp.concatenate(bases, axis=0), source[TGT_DEV:, span], last, FIT_PARTS)
            if d == 0 and step == 0:
                normal[...] = matrix
                right[...] = sides
            else:
                normal[...] += matrix
                right[...] += sides

    def solve():
        matrix = [normal[Z_DEV * p : Z_DEV * (p + 1), :] for p in range(len(pair_first))]
        sides = [right[Z_DEV * b : Z_DEV * (b + 1), :] for b in range(basis_count)]
        gain_out[...] = solve_normal(matrix, jnp.stack(sides))

    make_member(0)
    make_member(1)
    prepare(0)
    pl.semaphore_wait(barrier, len(near))
    copies[0][0].start()
    for p in range(1, AHEAD):
        prepare(p)
        copies[p][0].start()
    prepare(AHEAD)
    middle = basis_count // 2
    jobs = [
        functools.partial(make_windows, 0, middle), functools.partial(make_windows, middle, basis_count)
    ]
    jobs += [send_sums] + [functools.partial(fit_block, d, h) for d in range(bands) for h in range(2)] + [solve]
    for p in range(pieces + 3):
        if p < pieces:
            round_1(p)
            if p + AHEAD + 1 < pieces:
                prepare(p + AHEAD + 1)
        if 1 <= p <= pieces:
            round_2(p - 1)
        if p >= 3:
            round_3(p - 3)
        for repeat in range((0, 1, 1, 0, 2, 2, 2)[p] if p < 7 else 1):
            if jobs:
                jobs.pop(0)()
    for step in b_copies + [step for piece in copies for step in piece]:
        step.wait_send()


def finish_kernel(flux, res, gain, flux_out, res_out, gain_out):
    flux_out[...] = flux[...]
    res_out[...] = res[...]
    gain_out[...] = gain[...]


def dense_shards(
    exposure_flux, exposure_ivar, exposure_res, target_of_row, valid_of_row, rest_basis, redshift_shift
):
    owners = lax.axis_size("tgt")
    bands = lax.axis_size("band")
    rows, wave_dev = exposure_flux.shape
    waves = wave_dev * bands
    basis_count = rest_basis.shape[0]
    pair_rows = Z_DEV * (len(pair_first) + 1)
    vmem = pl.BlockSpec(memory_space=pltpu.VMEM)
    smem = pl.BlockSpec(memory_space=pltpu.SMEM)
    hbm = pl.BlockSpec(memory_space=pl.ANY)
    half, full = jnp.bfloat16, jnp.float32
    block = (TGT_DEV, wave_dev)
    count = owners * TGT_DEV
    pieces = NDIAG + 2
    buffers = []
    for r in range(3):
        shape = (pieces, count >> (r + 1), wave_dev)
        buffers += [pltpu.VMEM(shape, half), pltpu.VMEM(shape, half), pltpu.VMEM(shape, full)]
    dma = pltpu.SemaphoreType.DMA
    coadd_flux, coadd_res, gain = pl.pallas_call(
        fused_kernel,
        out_shape=(
            jax.ShapeDtypeStruct(block, full),
            jax.ShapeDtypeStruct((NDIAG,) + block, half),
            jax.ShapeDtypeStruct((Z_DEV, TGT_DEV), full),
        ),
        in_specs=[smem, vmem, vmem, vmem, hbm, hbm, hbm],
        out_specs=(vmem, vmem, vmem),
        scratch_shapes=[
            pltpu.VMEM((rows, wave_dev), half),
            pltpu.VMEM((rows, wave_dev), half),
            pltpu.VMEM((NDIAG, rows, wave_dev), half),
            pltpu.VMEM((rows, wave_dev), full),
            pltpu.VMEM((2, count, 2 * rows), half),
            pltpu.VMEM((basis_count, Z_DEV, waves), full),
        ] + buffers + [
            pltpu.VMEM((2 * TGT_DEV, wave_dev), half),
            pltpu.VMEM((bands - 1, 2 * TGT_DEV, wave_dev), half),
            pltpu.VMEM((pair_rows, TGT_DEV), full),
            pltpu.VMEM((Z_DEV * basis_count, TGT_DEV), full),
            pltpu.VMEM(block, full),
            dma((pieces,)),
            dma((pieces, 3)),
            dma((pieces, 3)),
            dma((bands - 1,)),
            dma((bands - 1,)),
        ],
        compiler_params=pltpu.CompilerParams(
            vmem_limit_bytes=VMEM_LIMIT, collective_id=0, has_side_effects=True
        ),
        name="coadd_and_fit",
    )(
        redshift_shift,
        target_of_row.reshape(owners, rows), valid_of_row.reshape(owners, rows), rest_basis,
        exposure_ivar, exposure_flux, jnp.transpose(exposure_res, (1, 0, 2)),
    )
    coadd_flux, coadd_res, gain = pl.pallas_call(
        finish_kernel,
        out_shape=(
            jax.ShapeDtypeStruct(block, full),
            jax.ShapeDtypeStruct(coadd_res.shape, half),
            jax.ShapeDtypeStruct(gain.shape, full),
        ),
        in_specs=[vmem] * 3,
        out_specs=(vmem, vmem, vmem),
        compiler_params=pltpu.CompilerParams(vmem_limit_bytes=VMEM_LIMIT),
        name="finish",
    )(coadd_flux, coadd_res, gain)
    return (coadd_flux, jnp.transpose(coadd_res, (1, 0, 2)), gain.T)


def solution(mesh):
    in_specs = (P("tgt", "band"), P("tgt", "band"), P("tgt", None, "band"), P(), P(), P(), P())
    out_specs = (P("tgt", "band"), P("tgt", None, "band"), P("tgt", "band"))
    owners = mesh.shape["tgt"]

    def whole(*args):
        rows = args[0].shape[0] // owners
        body = dense_shards if owners * TGT_DEV <= 2 * rows and owners == 8 else shards
        return jax.shard_map(
            body, mesh=mesh, in_specs=in_specs, out_specs=out_specs, check_vma=False
        )(*args)

    return whole
```
